768 devices in a mesh: dp: 32 (over x, y), expert: 4 (over z_hi), tensor: 6 (over z_lo, core).
Axes of the slice: x: 4, y: 8, z: 12 (z_hi: 4, z_lo: 3; z = z_hi * 3 + z_lo), core: 2. Of those that a mesh axis runs over, the one named last changes fastest.
Arguments:
- grad_out: bfloat16 [6144, 7168], P(('dp', 'expert')), may hold values from -24 to 24
- gate_prob: bfloat16 [6144, 2], P(('dp', 'expert')), may hold values from 0.049804688 to 0.94921875
- expert_ids: int32 [6144, 2], P(('dp', 'expert')), may hold values from 0 to 3, as said below
- slot_positions: int32 [6144, 2], P(('dp', 'expert')), may hold values from 0 to 38, as said below
- expert_down: bfloat16 [4, 2496, 7168], P('expert', 'tensor'), may hold values from -0.03125 to 0.03125
- dense_down: bfloat16 [2496, 7168], P(('expert', 'tensor')), may hold values from -0.03125 to 0.03125
- expert_gate_pre: bfloat16 [4, 4992, 2496], P('expert', 'dp', 'tensor'), may hold values from -6 to 6
- expert_up_pre: bfloat16 [4, 4992, 2496], P('expert', 'dp', 'tensor'), may hold values from -6 to 6
- dense_gate_pre: bfloat16 [6144, 2496], P('dp', ('expert', 'tensor')), may hold values from -6 to 6
- dense_up_pre: bfloat16 [6144, 2496], P('dp', ('expert', 'tensor')), may hold values from -6 to 6
Outputs:
- expert_gate_grad: bfloat16 [4, 4992, 2496], P('expert', 'dp', 'tensor')
- expert_up_grad: bfloat16 [4, 4992, 2496], P('expert', 'dp', 'tensor')
- slot_prob_grad: float32 [4, 4992], P('expert', 'dp')
- expert_down_grad: bfloat16 [4, 7168, 2496], P('expert', 'dp', 'tensor')
- dense_gate_grad: bfloat16 [6144, 2496], P('dp', ('expert', 'tensor'))
- dense_up_grad: bfloat16 [6144, 2496], P('dp', ('expert', 'tensor'))
- dense_down_grad: bfloat16 [7168, 2496], P('dp', ('expert', 'tensor'))
The draws below stay inside these ranges and needn't reach their ends.
Inputs may be any that keep to these rules, and one draw needn't show every extreme that they name: `expert_ids`: the two experts of a token differ. In each block of 48 tokens of one index of dp and expert, no expert is named more than 39 times, and one expert is named exactly 39 times; it is the same expert in all 4 blocks of one dp index. `slot_positions`: the rank of an assignment among the assignments of its block of 48 tokens to the same expert, counting tokens in order and a token's first expert before its second.
All inputs are finite; a program needn't handle non-finite values.
Results may differ from the reference program's by a relative error of at most 0.024.
Values may be sent and summed in bfloat16 or wider, within the bound.
No kernel may reach another device: no remote copies, remote signals or barrier semaphores. Data moves between devices by JAX's collectives and lax.ppermute only.
A program may use at most 64 MiB of HBM per device.

```python
import jax
import jax.numpy as jnp
from jax import lax

D = 7168
HE = 2496
HD = 2496
TOK_DEV = 48
CAP = 39
EXPERTS = 4
SLOTS = 4992
TOKENS = 6144
N_DP = 32
N_EXPERT = 4


def routing_table(base_key):
    blocks = N_DP * N_EXPERT
    key_hot, key_perm, key_rot, key_first, key_second = jax.random.split(base_key, 5)
    hot_group = jax.random.randint(key_hot, (N_DP,), 0, N_EXPERT)
    hot_block = jnp.repeat(hot_group, N_EXPERT)[:, None]
    perm_keys = jax.random.split(key_perm, blocks)
    orders = jax.vmap(lambda one_key: jax.random.permutation(one_key, TOK_DEV))(perm_keys)
    ranks = jnp.argsort(orders, axis=1, stable=True).astype(jnp.int32)
    spread = N_EXPERT - 1
    rotation = jax.random.randint(key_rot, (blocks, 1), 0, spread)
    first_off = jax.random.randint(key_first, (blocks, TOK_DEV), 0, spread)
    second_off = jax.random.randint(key_second, (blocks, TOK_DEV), 0, spread - 1)
    hot_rank = ranks < CAP
    offset_one = jnp.where(hot_rank, 0, 1 + first_off)
    offset_two = jnp.where(hot_rank, 1 + (ranks + rotation) % spread, 1 + (first_off + 1 + second_off) % spread)
    chosen = jnp.stack([(hot_block + offset_one) % N_EXPERT, (hot_block + offset_two) % N_EXPERT], axis=-1).astype(jnp.int32)
    flat = chosen.reshape(blocks, 2 * TOK_DEV)
    onehot = (flat[:, :, None] == jnp.arange(N_EXPERT, dtype=jnp.int32)[None, None, :]).astype(jnp.int32)
    before = jnp.cumsum(onehot, axis=1) - onehot
    slots = jnp.sum(before * onehot, axis=-1).astype(jnp.int32)
    return (chosen.reshape(TOKENS, 2), slots.reshape(TOKENS, 2))


def draw_expert_ids(key, part):
    chosen, slots = routing_table(key)
    return chosen


def draw_slot_positions(key, part):
    chosen, slots = routing_table(key)
    return slots


def with_spikes(values, own_key, source, target, parts, factor):
    owner, partner = [(jnp.arange(values.shape[dim]) // (values.shape[dim] // parts)).reshape([-1 if axis == dim else 1 for axis in range(values.ndim)]) for dim in (source, target)]
    chosen = jax.random.permutation(own_key, parts)[partner]
    strong = (owner == chosen) | (owner == (partner + parts // 2) % parts)
    return jnp.where(strong, factor * values, values)


def steps_of(rng, dims, cuts, smallest, largest):
    level = 1.0
    for axis_at, shards_of in cuts:
        heights = jax.random.uniform(jax.random.fold_in(jax.random.fold_in(rng, 6), axis_at), (shards_of,), jnp.float32, smallest / len(cuts), largest / len(cuts))
        level = level * jnp.repeat(jnp.exp(heights), dims[axis_at] // shards_of).reshape((-1,) + (1,) * (len(dims) - 1 - axis_at))
    return level


def centred(own_key, extent, scale, bound, shards=(), kind=jnp.bfloat16):
    gain = steps_of(own_key, extent, shards, -0.22, 0.18) if shards else 1.0
    result = jax.random.normal(own_key, extent, jnp.float32) * scale * gain
    return jnp.minimum(jnp.maximum(result, -bound), bound).astype(kind)


def bell_draw_with(rng, dims, deviation, reach, cuts, heavy, kind=jnp.bfloat16):
    drawn = deviation * jax.random.normal(rng, dims, jnp.float32)
    if cuts:
        drawn = drawn * steps_of(rng, dims, cuts, -0.22, 0.18)
    return jnp.clip(with_spikes(drawn, jax.random.fold_in(rng, 3), *heavy), -reach, reach).astype(kind)


def setup_inputs(seed: int = 0) -> dict:
    seeds = jax.random.split(jax.random.key(seed), 11)
    return {
        "grad_out": bell_draw_with(seeds[0], (TOKENS, D), 1.0, 24.0, ((0, 128),), (0, 1, 128, 5.5)),
        "gate_prob": jnp.clip(0.049804688 + 0.89941406 * jax.random.uniform(seeds[1], (TOKENS, 2), jnp.float32) ** steps_of(seeds[1], (TOKENS, 2), ((0, 128),), -0.2, 0.2), 0.049804688, 0.94921875).astype(jnp.bfloat16),
        "expert_ids": draw_expert_ids(jax.random.fold_in(seeds[10], 71), 0),
        "slot_positions": draw_slot_positions(jax.random.fold_in(seeds[10], 71), 0),
        "expert_down": centred(seeds[4], (EXPERTS, HE, D), (4 * D) ** -0.5, 0.03125, ((0, 4), (1, 6))),
        "dense_down": centred(seeds[5], (HD, D), (4 * D) ** -0.5, 0.03125, ((0, 24),)),
        "expert_gate_pre": centred(seeds[6], (EXPERTS, SLOTS, HE), 1.5, 6.0, ((0, 4), (1, 32), (2, 6))),
        "expert_up_pre": centred(seeds[7], (EXPERTS, SLOTS, HE), 1.0, 6.0, ((0, 4), (1, 32), (2, 6))),
        "dense_gate_pre": centred(seeds[8], (TOKENS, HD), 1.5, 6.0, ((0, 32), (1, 24))),
        "dense_up_pre": centred(seeds[9], (TOKENS, HD), 1.0, 6.0, ((0, 32), (1, 24))),
    }


def silu_parts(gate_val):
    gate_sig = jax.nn.sigmoid(gate_val)
    activated = gate_val * gate_sig
    slope = gate_sig * (1.0 + gate_val * (1.0 - gate_sig))
    return activated, slope


def replica_sum(rows_in, weighted):
    rows_split = rows_in.reshape(N_DP, -1, rows_in.shape[1])
    weighted_split = weighted.reshape(N_DP, -1, weighted.shape[1])

    def add_term(summed, pair):
        term = jnp.dot(pair[0].T, pair[1], preferred_element_type=jnp.float32)
        rounded = lax.optimization_barrier(term.astype(jnp.bfloat16))
        return summed + rounded.astype(jnp.float32), None

    start_sum = jnp.zeros((rows_in.shape[1], weighted.shape[1]), jnp.float32)
    summed, _ = lax.scan(add_term, start_sum, (rows_split, weighted_split))
    return (summed / N_DP).astype(jnp.bfloat16)


def reference(grad_out, gate_prob, expert_ids, slot_positions, expert_down, dense_down, expert_gate_pre, expert_up_pre, dense_gate_pre, dense_up_pre):
    block_index = jnp.arange(TOKENS, dtype=jnp.int32) // TOK_DEV
    row_index = (block_index[:, None] * CAP + slot_positions).astype(jnp.int32)
    routed = jnp.zeros((EXPERTS, SLOTS, D), jnp.bfloat16).at[expert_ids, row_index].set(
        jnp.broadcast_to(grad_out[:, None, :], (TOKENS, 2, D)))
    routed_prob = jnp.zeros((EXPERTS, SLOTS), jnp.float32).at[expert_ids, row_index].set(
        gate_prob.astype(jnp.float32))

    def one_expert(inputs):
        rows_in, prob_in, weight_in, gate_in, up_in = inputs
        back_hidden = jnp.dot(rows_in, weight_in.T, preferred_element_type=jnp.float32)
        gate_val = gate_in.astype(jnp.float32)
        up_val = up_in.astype(jnp.float32)
        activated, slope = silu_parts(gate_val)
        hidden = activated * up_val
        dots = jnp.sum(back_hidden * hidden, axis=1)
        scaled = prob_in[:, None] * back_hidden
        gate_grad = (scaled * up_val * slope).astype(jnp.bfloat16)
        up_grad = (scaled * activated).astype(jnp.bfloat16)
        weighted = (prob_in[:, None] * hidden).astype(jnp.bfloat16)
        down_grad = replica_sum(rows_in, weighted)
        return gate_grad, up_grad, dots, down_grad

    expert_gate_grad, expert_up_grad, slot_prob_grad, expert_down_grad = lax.map(
        one_expert, (routed, routed_prob, expert_down, expert_gate_pre, expert_up_pre))

    back_dense = jnp.dot(grad_out, dense_down.T, preferred_element_type=jnp.float32)
    dense_gate = dense_gate_pre.astype(jnp.float32)
    dense_up = dense_up_pre.astype(jnp.float32)
    dense_act, dense_slope = silu_parts(dense_gate)
    dense_gate_grad = (back_dense * dense_up * dense_slope).astype(jnp.bfloat16)
    dense_up_grad = (back_dense * dense_act).astype(jnp.bfloat16)
    dense_hidden = (dense_act * dense_up).astype(jnp.bfloat16)
    dense_down_grad = replica_sum(grad_out, dense_hidden)
    return (expert_gate_grad, expert_up_grad, slot_prob_grad, expert_down_grad,
            dense_gate_grad, dense_up_grad, dense_down_grad)
```

```python
import functools

import jax
import jax.numpy as jnp
from jax import lax
from jax.experimental import pallas as pl
from jax.experimental.pallas import tpu as pltpu
from jax.sharding import Mesh
from jax.sharding import PartitionSpec as P

X_CHIPS = 4
RUN = 3
CORES = 2
LANES = 128
SLOT_ROWS = 160
VMEM_BYTES = 56 * 1024 * 1024


def silu_parts(gate_val):
    gate_sig = jax.nn.sigmoid(gate_val)
    activated = gate_val * gate_sig
    slope = gate_sig * (1.0 + gate_val * (1.0 - gate_sig))
    return (activated, slope)


def whole(*shape):
    return pl.BlockSpec(shape, lambda *idx: (0,) * len(shape))


def params():
    return pltpu.CompilerParams(vmem_limit_bytes=VMEM_BYTES)


def hidden_kernel(gate_ref, up_ref, dgate_ref, dup_ref, out_ref):
    slots, width = gate_ref.shape[1:]
    tokens, dwidth = dgate_ref.shape
    quarter = tokens // 4
    out_ref[...] = jnp.zeros_like(out_ref)
    activated, _ = silu_parts(gate_ref[0].astype(jnp.float32))
    hidden = activated * up_ref[0].astype(jnp.float32)
    pad = jnp.zeros((SLOT_ROWS - slots, width), jnp.float32)
    out_ref[:SLOT_ROWS, :width] = jnp.concatenate([hidden, pad], axis=0).astype(jnp.bfloat16)
    dactivated, _ = silu_parts(dgate_ref[...].astype(jnp.float32))
    dhidden = (dactivated * dup_ref[...].astype(jnp.float32)).astype(jnp.bfloat16)
    for j in range(4):
        out_ref[SLOT_ROWS : SLOT_ROWS + quarter, j * LANES : j * LANES + dwidth] = dhidden[
            j * quarter : (j + 1) * quarter
        ]


def split_kernel(nx, ny, rows_ref, out_ref):
    width = rows_ref.shape[1] - LANES
    block = width // (nx * ny)
    for y in range(ny):
        for x in range(nx):
            at = (x * ny + y) * block
            out_ref[y, :, x * block : (x + 1) * block] = rows_ref[:, at : at + block]
        out_ref[y, :, nx * block :] = rows_ref[:, width:]


def routing(meta, expert):
    hit0 = meta[:, 0:1] == expert
    hit1 = meta[:, 1:2] == expert
    slot = jnp.where(hit0, meta[:, 2:3], jnp.where(hit1, meta[:, 3:4], -1.0)).astype(jnp.int32)
    prob = jnp.where(hit0, meta[:, 4:5], jnp.where(hit1, meta[:, 5:6], 0.0))
    token = meta[:, 6:7].astype(jnp.int32)
    return slot, prob, token


def one_hot(index, count, value=1.0):
    lane = lax.broadcasted_iota(jnp.int32, (index.shape[0], count), 1)
    return jnp.where(lane == index, value, 0.0).astype(jnp.bfloat16)


def dot(a, b, dims):
    return lax.dot_general(a, b, (dims, ((), ())), preferred_element_type=jnp.float32)


def weight_kernel(width, dwidth, expert_ref, *refs):
    pieces, hid_ref, out_ref, a_ref, b_ref = refs[:6], refs[6], refs[7], refs[8], refs[9]
    ny, rows, total = pieces[0].shape
    cols = total - LANES
    group = 6 * rows
    expert = expert_ref[0].astype(jnp.float32)
    quarter = hid_ref.shape[1] - SLOT_ROWS
    base = out_ref.shape[2] - LANES
    b_ref[...] = jnp.zeros_like(b_ref)
    for y in range(ny):
        top = y * group
        for i, piece in enumerate(pieces):
            a_ref[top + i * rows : top + (i + 1) * rows, :] = piece[y, :, :cols]
        meta = jnp.concatenate([piece[y, :, cols:] for piece in pieces], axis=0).astype(jnp.float32)
        slot, prob, token = routing(meta, expert)
        weighted = dot(one_hot(slot, SLOT_ROWS, prob), hid_ref[y, :SLOT_ROWS, :width], ((1,), (0,)))
        b_ref[top : top + group, :width] = weighted.astype(jnp.bfloat16)
        dense = jnp.concatenate(
            [hid_ref[y, SLOT_ROWS:, j * LANES : (j + 1) * LANES] for j in range(4)], axis=0
        )
        moved = dot(one_hot(token, 4 * quarter), dense, ((1,), (0,)))
        b_ref[top : top + group, base : base + LANES] = moved.astype(jnp.bfloat16)
    summed = dot(a_ref[...], b_ref[...], ((0,), (0,))).astype(jnp.bfloat16)
    block = out_ref.shape[1]
    for x in range(out_ref.shape[0]):
        out_ref[x] = summed[x * block : (x + 1) * block]


def sum_kernel(scale, in_ref, expert_ref, dense_ref):
    summed = in_ref[0].astype(jnp.float32)
    for x in range(1, in_ref.shape[0]):
        summed = summed + in_ref[x].astype(jnp.float32)
    summed = (summed * scale).astype(jnp.bfloat16)
    base = in_ref.shape[2] - LANES
    expert_ref[0] = summed[:, : expert_ref.shape[2]]
    dense_ref[...] = summed[:, base : base + dense_ref.shape[1]]


def place(onehot, values):
    high = values.astype(jnp.bfloat16)
    rest = values - high.astype(jnp.float32)
    middle = rest.astype(jnp.bfloat16)
    low = (rest - middle.astype(jnp.float32)).astype(jnp.bfloat16)
    dims = ((0,), (0,))
    return dot(onehot, high, dims) + dot(onehot, middle, dims) + dot(onehot, low, dims)


def back_kernel(expert_ref, *refs):
    datas, metas = refs[:6], refs[6:12]
    we_ref, wd_ref, gate_ref, up_ref, dgate_ref, dup_ref = refs[12:18]
    gate_out, up_out, dots_out, dgate_out, dup_out = refs[18:23]
    acc_e, acc_d = refs[23:25]
    step = pl.program_id(0)

    @pl.when(step == 0)
    def _():
        acc_e[...] = jnp.zeros_like(acc_e)
        acc_d[...] = jnp.zeros_like(acc_d)

    rows = jnp.concatenate([data[...] for data in datas], axis=0)
    acc_e[...] += dot(rows, we_ref[0], ((1,), (1,)))
    acc_d[...] += dot(rows, wd_ref[...], ((1,), (1,)))

    @pl.when(step == pl.num_programs(0) - 1)
    def _():
        meta = jnp.concatenate([m[...] for m in metas], axis=0).astype(jnp.float32)
        slot, prob, token = routing(meta, expert_ref[0].astype(jnp.float32))
        slots = gate_ref.shape[1]
        hot = one_hot(slot, slots)
        back = place(hot, acc_e[...])
        wide = jnp.broadcast_to(prob, (prob.shape[0], LANES)).astype(jnp.bfloat16)
        slot_prob = dot(hot, wide, ((0,), (0,)))[:, :1]
        up_val = up_ref[0].astype(jnp.float32)
        activated, slope = silu_parts(gate_ref[0].astype(jnp.float32))
        product = back * (activated * up_val)
        ones = jnp.ones((8, product.shape[1]), jnp.float32)
        dots_out[...] = lax.dot_general(
            ones,
            product,
            (((1,), (1,)), ((), ())),
            precision=lax.Precision.HIGHEST,
            preferred_element_type=jnp.float32,
        )
        scaled = slot_prob * back
        gate_out[0] = (scaled * up_val * slope).astype(jnp.bfloat16)
        up_out[0] = (scaled * activated).astype(jnp.bfloat16)
        dback = place(one_hot(token, dgate_ref.shape[0]), acc_d[...])
        dactivated, dslope = silu_parts(dgate_ref[...].astype(jnp.float32))
        dgate_out[...] = (dback * dup_ref[...].astype(jnp.float32) * dslope).astype(jnp.bfloat16)
        dup_out[...] = (dback * dactivated).astype(jnp.bfloat16)


def ring(count, step):
    return [(i, (i + step) % count) for i in range(count)]


def local(
    grad_out,
    gate_prob,
    expert_ids,
    slot_positions,
    expert_down,
    dense_down,
    expert_gate_pre,
    expert_up_pre,
    dense_gate_pre,
    dense_up_pre,
):
    nx, ny, ne = lax.axis_size("x"), lax.axis_size("y"), lax.axis_size("e")
    expert, part = lax.axis_index("e"), lax.axis_index(("l", "c"))
    tokens, width = grad_out.shape
    slots, hwidth = expert_gate_pre.shape[1:]
    dwidth = dense_gate_pre.shape[1]
    capacity = slots // ne
    eighth = tokens // (RUN * CORES)
    block = width // (nx * ny)
    bf16 = jnp.bfloat16
    expert_arr = expert.reshape(1).astype(jnp.int32)
    smem = pl.BlockSpec(memory_space=pltpu.SMEM)

    hidden = pl.pallas_call(
        hidden_kernel,
        out_shape=jax.ShapeDtypeStruct((SLOT_ROWS + ne * tokens // 4, 4 * LANES), bf16),
        compiler_params=params(),
    )(expert_gate_pre, expert_up_pre, dense_gate_pre, dense_up_pre)
    hiddens = lax.all_gather(hidden, "y", axis=0)

    token = expert * tokens + lax.broadcasted_iota(jnp.int32, (tokens, 1), 0)
    meta = jnp.concatenate(
        [
            expert_ids.astype(bf16),
            (slot_positions + expert * capacity).astype(bf16),
            gate_prob,
            token.astype(bf16),
        ],
        axis=1,
    )
    meta = jnp.pad(meta, ((0, 0), (0, LANES - meta.shape[1])))
    mine = jnp.concatenate(
        [
            lax.dynamic_slice(grad_out, (part * eighth, 0), (eighth, width)),
            lax.dynamic_slice(meta, (part * eighth, 0), (eighth, LANES)),
        ],
        axis=1,
    )
    rows = lax.all_gather(mine, "e", axis=0, tiled=True)

    chunks = pl.pallas_call(
        functools.partial(split_kernel, nx, ny),
        out_shape=jax.ShapeDtypeStruct((ny, ne * eighth, nx * block + LANES), bf16),
        compiler_params=params(),
    )(rows)
    chunks = lax.all_to_all(chunks, "y", split_axis=0, concat_axis=0, tiled=True)

    def spread(piece):
        along = [piece] + [lax.ppermute(piece, ("e", "l"), ring(ne * RUN, d)) for d in (1, -1)]
        other = [lax.ppermute(p, "c", ring(CORES, 1)) for p in along]
        return along + other

    row_pieces = spread(rows)
    chunk_pieces = spread(chunks)

    cols = hwidth + (-hwidth) % LANES + LANES
    ktotal = ny * 6 * ne * eighth
    partial_sums = pl.pallas_call(
        functools.partial(weight_kernel, hwidth, dwidth),
        out_shape=jax.ShapeDtypeStruct((nx, block, cols), bf16),
        in_specs=[smem] + [pl.BlockSpec(memory_space=pltpu.VMEM)] * 7,
        scratch_shapes=[
            pltpu.VMEM((ktotal, nx * block), bf16),
            pltpu.VMEM((ktotal, cols), bf16),
        ],
        compiler_params=params(),
    )(expert_arr, *chunk_pieces, hiddens)
    landed = lax.all_to_all(partial_sums, "x", split_axis=0, concat_axis=0, tiled=True)
    expert_down_grad, dense_down_grad = pl.pallas_call(
        functools.partial(sum_kernel, 1.0 / (nx * ny)),
        out_shape=(
            jax.ShapeDtypeStruct((1, block, hwidth), bf16),
            jax.ShapeDtypeStruct((block, dwidth), bf16),
        ),
        compiler_params=params(),
    )(landed)

    depth = 1024
    data_spec = pl.BlockSpec((ne * eighth, depth), lambda k: (0, k))
    meta_spec = pl.BlockSpec((ne * eighth, LANES), lambda k: (0, width // LANES))
    gate_grad, up_grad, dots, dense_gate_grad, dense_up_grad = pl.pallas_call(
        back_kernel,
        grid=(width // depth,),
        out_shape=(
            jax.ShapeDtypeStruct((1, slots, hwidth), bf16),
            jax.ShapeDtypeStruct((1, slots, hwidth), bf16),
            jax.ShapeDtypeStruct((8, slots), jnp.float32),
            jax.ShapeDtypeStruct((ne * tokens, dwidth), bf16),
            jax.ShapeDtypeStruct((ne * tokens, dwidth), bf16),
        ),
        in_specs=[smem]
        + [data_spec] * 6
        + [meta_spec] * 6
        + [
            pl.BlockSpec((1, hwidth, depth), lambda k: (0, 0, k)),
            pl.BlockSpec((dwidth, depth), lambda k: (0, k)),
            whole(1, slots, hwidth),
            whole(1, slots, hwidth),
            whole(ne * tokens, dwidth),
            whole(ne * tokens, dwidth),
        ],
        out_specs=(
            whole(1, slots, hwidth),
            whole(1, slots, hwidth),
            whole(8, slots),
            whole(ne * tokens, dwidth),
            whole(ne * tokens, dwidth),
        ),
        scratch_shapes=[
            pltpu.VMEM((ne * tokens, hwidth), jnp.float32),
            pltpu.VMEM((ne * tokens, dwidth), jnp.float32),
        ],
        compiler_params=params(),
    )(
        expert_arr,
        *row_pieces,
        *row_pieces,
        expert_down,
        dense_down,
        expert_gate_pre,
        expert_up_pre,
        dense_gate_pre,
        dense_up_pre,
    )
    slot_prob_grad = lax.psum(dots[:1], ("l", "c"))
    return (
        gate_grad,
        up_grad,
        slot_prob_grad,
        expert_down_grad,
        dense_gate_grad,
        dense_up_grad,
        dense_down_grad,
    )


def solution(mesh):
    n_dp, n_expert, n_tensor = (mesh.shape[a] for a in ("dp", "expert", "tensor"))
    fine = Mesh(
        mesh.devices.reshape(X_CHIPS, n_dp // X_CHIPS, n_expert, n_tensor // CORES, CORES),
        ("x", "y", "e", "l", "c"),
    )
    dp, tensor = ("x", "y"), ("l", "c")
    return jax.shard_map(
        local,
        mesh=fine,
        in_specs=(
            P((*dp, "e"), None),
            P((*dp, "e"), None),
            P((*dp, "e"), None),
            P((*dp, "e"), None),
            P("e", tensor, None),
            P(("e", *tensor), None),
            P("e", dp, tensor),
            P("e", dp, tensor),
            P(dp, ("e", *tensor)),
            P(dp, ("e", *tensor)),
        ),
        out_specs=(
            P("e", dp, tensor),
            P("e", dp, tensor),
            P("e", dp),
            P("e", dp, tensor),
            P(dp, ("e", *tensor)),
            P(dp, ("e", *tensor)),
            P(dp, ("e", *tensor)),
        ),
        check_vma=False,
    )
```

```python
import functools

import jax
import jax.numpy as jnp
from jax import lax
from jax.experimental import pallas as pl
from jax.experimental.pallas import tpu as pltpu
from jax.sharding import Mesh
from jax.sharding import PartitionSpec as P

X_CHIPS = 4
RUN = 3
CORES = 2
LANES = 128
SLOT_ROWS = 160
VMEM_BYTES = 56 * 1024 * 1024


def silu_parts(gate_val):
    gate_sig = jax.nn.sigmoid(gate_val)
    activated = gate_val * gate_sig
    slope = gate_sig * (1.0 + gate_val * (1.0 - gate_sig))
    return (activated, slope)


def whole(*shape):
    return pl.BlockSpec(shape, lambda *idx: (0,) * len(shape))


def params():
    return pltpu.CompilerParams(vmem_limit_bytes=VMEM_BYTES)


def hidden_kernel(gate_ref, up_ref, dgate_ref, dup_ref, out_ref):
    slots, width = gate_ref.shape[1:]
    tokens, dwidth = dgate_ref.shape
    quarter = tokens // 4
    out_ref[...] = jnp.zeros_like(out_ref)
    activated, _ = silu_parts(gate_ref[0].astype(jnp.float32))
    hidden = activated * up_ref[0].astype(jnp.float32)
    pad = jnp.zeros((SLOT_ROWS - slots, width), jnp.float32)
    out_ref[:SLOT_ROWS, :width] = jnp.concatenate([hidden, pad], axis=0).astype(jnp.bfloat16)
    dactivated, _ = silu_parts(dgate_ref[...].astype(jnp.float32))
    dhidden = (dactivated * dup_ref[...].astype(jnp.float32)).astype(jnp.bfloat16)
    for j in range(4):
        out_ref[SLOT_ROWS : SLOT_ROWS + quarter, j * LANES : j * LANES + dwidth] = dhidden[
            j * quarter : (j + 1) * quarter
        ]


def pick_kernel(capacity, at_ref, rows_ref, prob_ref, ids_ref, slots_ref, out_ref):
    expert, part = at_ref[0], at_ref[1]
    eighth = out_ref.shape[0]
    tokens, width = rows_ref.shape
    lane = lax.broadcasted_iota(jnp.int32, (eighth, tokens), 1)
    row = lax.broadcasted_iota(jnp.int32, (eighth, tokens), 0)
    chosen = jnp.where(lane == row + part * eighth, 1.0, 0.0).astype(jnp.bfloat16)
    out_ref[:, :width] = dot(chosen, rows_ref[...], ((1,), (0,))).astype(jnp.bfloat16)
    token = expert * tokens + lax.broadcasted_iota(jnp.int32, (2, tokens), 1)
    meta = jnp.concatenate(
        [
            ids_ref[...].astype(jnp.float32),
            (slots_ref[...] + expert * capacity).astype(jnp.float32),
            prob_ref[...].astype(jnp.float32),
            token.astype(jnp.float32),
        ],
        axis=0,
    ).astype(jnp.bfloat16)
    meta = jnp.concatenate([meta, jnp.zeros((LANES - 8, tokens), jnp.bfloat16)], axis=0)
    out_ref[:, width:] = dot(chosen, meta, ((1,), (1,))).astype(jnp.bfloat16)


def split_kernel(nx, ny, rows_ref, out_ref):
    width = rows_ref.shape[1] - LANES
    block = width // (nx * ny)
    stride = out_ref.shape[2] // nx
    for y in range(ny):
        for x in range(nx):
            at = (x * ny + y) * block
            out_ref[y, :, x * stride : x * stride + block] = rows_ref[:, at : at + block]
            out_ref[y, :, x * stride + block : (x + 1) * stride] = rows_ref[
                :, width : width + stride - block
            ]


def routing(meta, expert):
    hit0 = meta[:, 0:1] == expert
    hit1 = meta[:, 1:2] == expert
    slot = jnp.where(hit0, meta[:, 2:3], jnp.where(hit1, meta[:, 3:4], -1.0)).astype(jnp.int32)
    prob = jnp.where(hit0, meta[:, 4:5], jnp.where(hit1, meta[:, 5:6], 0.0))
    token = meta[:, 6:7].astype(jnp.int32)
    return slot, prob, token


def one_hot(index, count, value=1.0):
    lane = lax.broadcasted_iota(jnp.int32, (index.shape[0], count), 1)
    return jnp.where(lane == index, value, 0.0).astype(jnp.bfloat16)


def dot(a, b, dims):
    return lax.dot_general(a, b, (dims, ((), ())), preferred_element_type=jnp.float32)


def weight_kernel(block, expert_ref, *refs):
    pieces, hid_ref, out_ref, a_ref, be_ref, bd_ref = refs[:6], *refs[6:11]
    ny, rows, _ = pieces[0].shape
    group = 6 * rows
    expert = expert_ref[0].astype(jnp.float32)
    width = be_ref.shape[1]
    quarter = hid_ref.shape[1] - SLOT_ROWS
    for y in range(ny):
        top = y * group
        for i, piece in enumerate(pieces):
            a_ref[top + i * rows : top + (i + 1) * rows, :] = piece[y]
        meta = jnp.concatenate([piece[y, :, block : block + 8] for piece in pieces], axis=0)
        slot, prob, token = routing(meta.astype(jnp.float32), expert)
        weighted = dot(one_hot(slot, SLOT_ROWS, prob), hid_ref[y, :SLOT_ROWS, :width], ((1,), (0,)))
        be_ref[top : top + group, :] = weighted.astype(jnp.bfloat16)
        dense = jnp.concatenate(
            [hid_ref[y, SLOT_ROWS:, j * LANES : (j + 1) * LANES] for j in range(4)], axis=0
        )
        moved = dot(one_hot(token, 4 * quarter), dense, ((1,), (0,)))
        bd_ref[top : top + group, :] = moved.astype(jnp.bfloat16)
    rows_in = a_ref[...]
    nx, height, stride = out_ref.shape
    summed = dot(be_ref[...], rows_in, ((0,), (0,))).astype(jnp.bfloat16)
    dsummed = dot(bd_ref[...], rows_in, ((0,), (0,))).astype(jnp.bfloat16)
    for x in range(nx):
        out_ref[x, :width, :] = summed[:, x * stride : (x + 1) * stride]
        out_ref[x, width:, :] = dsummed[: height - width, x * stride : (x + 1) * stride]


def sum_kernel(scale, in_ref, expert_ref, dense_ref):
    summed = in_ref[0].astype(jnp.float32)
    for x in range(1, in_ref.shape[0]):
        summed = summed + in_ref[x].astype(jnp.float32)
    summed = (summed * scale).astype(jnp.bfloat16)
    width, block = expert_ref.shape
    expert_ref[...] = summed[:width, :block]
    dense_ref[...] = summed[width : width + dense_ref.shape[0], :block]


def place(onehot, values):
    high = values.astype(jnp.bfloat16)
    rest = values - high.astype(jnp.float32)
    middle = rest.astype(jnp.bfloat16)
    low = (rest - middle.astype(jnp.float32)).astype(jnp.bfloat16)
    dims = ((0,), (0,))
    return dot(onehot, high, dims) + dot(onehot, middle, dims) + dot(onehot, low, dims)


def back_kernel(expert_ref, *refs):
    datas, metas = refs[:6], refs[6:12]
    we_ref, wd_ref, gate_ref, up_ref, dgate_ref, dup_ref = refs[12:18]
    gate_out, up_out, dots_out, dgate_out, dup_out = refs[18:23]
    acc_e, acc_d = refs[23:25]
    step = pl.program_id(0)

    @pl.when(step == 0)
    def _():
        acc_e[...] = jnp.zeros_like(acc_e)
        acc_d[...] = jnp.zeros_like(acc_d)

    rows = jnp.concatenate([data[...] for data in datas], axis=0)
    acc_e[...] += dot(rows, we_ref[0], ((1,), (1,)))
    acc_d[...] += dot(rows, wd_ref[...], ((1,), (1,)))

    @pl.when(step == pl.num_programs(0) - 1)
    def _():
        meta = jnp.concatenate([m[...] for m in metas], axis=0).astype(jnp.float32)
        slot, prob, token = routing(meta, expert_ref[0].astype(jnp.float32))
        slots = gate_ref.shape[1]
        hot = one_hot(slot, slots)
        back = place(hot, acc_e[...])
        wide = jnp.broadcast_to(prob, (prob.shape[0], LANES)).astype(jnp.bfloat16)
        slot_prob = dot(hot, wide, ((0,), (0,)))[:, :1]
        up_val = up_ref[0].astype(jnp.float32)
        activated, slope = silu_parts(gate_ref[0].astype(jnp.float32))
        product = back * (activated * up_val)
        ones = jnp.ones((8, product.shape[1]), jnp.float32)
        dots_out[...] = lax.dot_general(
            ones,
            product,
            (((1,), (1,)), ((), ())),
            precision=lax.Precision.HIGHEST,
            preferred_element_type=jnp.float32,
        )
        scaled = slot_prob * back
        gate_out[0] = (scaled * up_val * slope).astype(jnp.bfloat16)
        up_out[0] = (scaled * activated).astype(jnp.bfloat16)
        dback = place(one_hot(token, dgate_ref.shape[0]), acc_d[...])
        dactivated, dslope = silu_parts(dgate_ref[...].astype(jnp.float32))
        dgate_out[...] = (dback * dup_ref[...].astype(jnp.float32) * dslope).astype(jnp.bfloat16)
        dup_out[...] = (dback * dactivated).astype(jnp.bfloat16)


def ring(count, step):
    return [(i, (i + step) % count) for i in range(count)]


def local(
    grad_out,
    gate_prob,
    expert_ids,
    slot_positions,
    expert_down,
    dense_down,
    expert_gate_pre,
    expert_up_pre,
    dense_gate_pre,
    dense_up_pre,
):
    nx, ny, ne = lax.axis_size("x"), lax.axis_size("y"), lax.axis_size("e")
    expert, part = lax.axis_index("e"), lax.axis_index(("l", "c"))
    tokens, width = grad_out.shape
    slots, hwidth = expert_gate_pre.shape[1:]
    dwidth = dense_gate_pre.shape[1]
    capacity = slots // ne
    eighth = tokens // (RUN * CORES)
    block = width // (nx * ny)
    bf16 = jnp.bfloat16
    stride = -(-(block + 8) // LANES) * LANES
    expert_arr = expert.reshape(1).astype(jnp.int32)
    smem = pl.BlockSpec(memory_space=pltpu.SMEM)
    vmem = pl.BlockSpec(memory_space=pltpu.VMEM)

    hidden = pl.pallas_call(
        hidden_kernel,
        out_shape=jax.ShapeDtypeStruct((SLOT_ROWS + ne * tokens // 4, 4 * LANES), bf16),
        compiler_params=params(),
    )(expert_gate_pre, expert_up_pre, dense_gate_pre, dense_up_pre)
    hiddens = lax.all_gather(hidden, "y", axis=0)

    mine = pl.pallas_call(
        functools.partial(pick_kernel, capacity),
        out_shape=jax.ShapeDtypeStruct((eighth, width + LANES), bf16),
        in_specs=[smem] + [vmem] * 4,
        compiler_params=params(),
    )(
        jnp.stack([expert, part]).astype(jnp.int32),
        grad_out,
        gate_prob.T,
        expert_ids.T,
        slot_positions.T,
    )
    rows = lax.all_gather(mine, "e", axis=0, tiled=True)

    chunks = pl.pallas_call(
        functools.partial(split_kernel, nx, ny),
        out_shape=jax.ShapeDtypeStruct((ny, ne * eighth, nx * stride), bf16),
        compiler_params=params(),
    )(rows)
    chunks = lax.all_to_all(chunks, "y", split_axis=0, concat_axis=0, tiled=True)

    def spread(piece):
        along = [piece] + [lax.ppermute(piece, ("e", "l"), ring(ne * RUN, d)) for d in (1, -1)]
        other = [lax.ppermute(p, "c", ring(CORES, 1)) for p in along]
        return along + other

    row_pieces = spread(rows)
    chunks, *row_pieces = lax.optimization_barrier((chunks, *row_pieces))
    chunk_pieces = spread(chunks)

    depth = 1024
    data_spec = pl.BlockSpec((ne * eighth, depth), lambda k: (0, k))
    meta_spec = pl.BlockSpec((ne * eighth, LANES), lambda k: (0, width // LANES))
    gate_grad, up_grad, dots, dense_gate_grad, dense_up_grad = pl.pallas_call(
        back_kernel,
        grid=(width // depth,),
        out_shape=(
            jax.ShapeDtypeStruct((1, slots, hwidth), bf16),
            jax.ShapeDtypeStruct((1, slots, hwidth), bf16),
            jax.ShapeDtypeStruct((8, slots), jnp.float32),
            jax.ShapeDtypeStruct((ne * tokens, dwidth), bf16),
            jax.ShapeDtypeStruct((ne * tokens, dwidth), bf16),
        ),
        in_specs=[smem]
        + [data_spec] * 6
        + [meta_spec] * 6
        + [
            pl.BlockSpec((1, hwidth, depth), lambda k: (0, 0, k)),
            pl.BlockSpec((dwidth, depth), lambda k: (0, k)),
            whole(1, slots, hwidth),
            whole(1, slots, hwidth),
            whole(ne * tokens, dwidth),
            whole(ne * tokens, dwidth),
        ],
        out_specs=(
            whole(1, slots, hwidth),
            whole(1, slots, hwidth),
            whole(8, slots),
            whole(ne * tokens, dwidth),
            whole(ne * tokens, dwidth),
        ),
        scratch_shapes=[
            pltpu.VMEM((ne * tokens, hwidth), jnp.float32),
            pltpu.VMEM((ne * tokens, dwidth), jnp.float32),
        ],
        compiler_params=params(),
    )(
        expert_arr,
        *row_pieces,
        *row_pieces,
        expert_down,
        dense_down,
        expert_gate_pre,
        expert_up_pre,
        dense_gate_pre,
        dense_up_pre,
    )

    expert_arr, dots = lax.optimization_barrier((expert_arr, dots))
    height = hwidth + -(-dwidth // 16) * 16
    ktotal = ny * ne * tokens
    partial_sums = pl.pallas_call(
        functools.partial(weight_kernel, block),
        out_shape=jax.ShapeDtypeStruct((nx, height, stride), bf16),
        in_specs=[smem] + [vmem] * 7,
        scratch_shapes=[
            pltpu.VMEM((ktotal, nx * stride), bf16),
            pltpu.VMEM((ktotal, hwidth), bf16),
            pltpu.VMEM((ktotal, LANES), bf16),
        ],
        compiler_params=params(),
    )(expert_arr, *chunk_pieces, hiddens)
    partial_sums, dots = lax.optimization_barrier((partial_sums, dots))
    landed = lax.all_to_all(partial_sums, "x", split_axis=0, concat_axis=0, tiled=True)
    slot_prob_grad = lax.psum(dots[:1], ("l", "c"))
    expert_down_grad, dense_down_grad = pl.pallas_call(
        functools.partial(sum_kernel, 1.0 / (nx * ny)),
        out_shape=(
            jax.ShapeDtypeStruct((hwidth, block), bf16),
            jax.ShapeDtypeStruct((dwidth, block), bf16),
        ),
        compiler_params=params(),
    )(landed)
    return (
        gate_grad,
        up_grad,
        slot_prob_grad,
        expert_down_grad.T[None],
        dense_gate_grad,
        dense_up_grad,
        dense_down_grad.T,
    )


def solution(mesh):
    n_dp, n_expert, n_tensor = (mesh.shape[a] for a in ("dp", "expert", "tensor"))
    fine = Mesh(
        mesh.devices.reshape(X_CHIPS, n_dp // X_CHIPS, n_expert, n_tensor // CORES, CORES),
        ("x", "y", "e", "l", "c"),
    )
    dp, tensor = ("x", "y"), ("l", "c")
    return jax.shard_map(
        local,
        mesh=fine,
        in_specs=(
            P((*dp, "e"), None),
            P((*dp, "e"), None),
            P((*dp, "e"), None),
            P((*dp, "e"), None),
            P("e", tensor, None),
            P(("e", *tensor), None),
            P("e", dp, tensor),
            P("e", dp, tensor),
            P(dp, ("e", *tensor)),
            P(dp, ("e", *tensor)),
        ),
        out_specs=(
            P("e", dp, tensor),
            P("e", dp, tensor),
            P("e", dp),
            P("e", dp, tensor),
            P(dp, ("e", *tensor)),
            P(dp, ("e", *tensor)),
            P(dp, ("e", *tensor)),
        ),
        check_vma=False,
    )
```

```python
import functools
import math

import jax
import jax.numpy as jnp
from jax import lax
from jax.experimental import pallas as pl
from jax.experimental.pallas import tpu as pltpu
from jax.sharding import Mesh
from jax.sharding import PartitionSpec as P

X_CHIPS = 4
RUN = 3
CORES = 2
LANES = 128
SLOT_ROWS = 160
VMEM_BYTES = 56 * 1024 * 1024


def silu_parts(gate_val):
    gate_sig = jax.nn.sigmoid(gate_val)
    activated = gate_val * gate_sig
    slope = gate_sig * (1.0 + gate_val * (1.0 - gate_sig))
    return (activated, slope)


def whole(*shape):
    return pl.BlockSpec(shape, lambda *idx: (0,) * len(shape))


def params():
    return pltpu.CompilerParams(vmem_limit_bytes=VMEM_BYTES)


def hidden_kernel(gate_ref, up_ref, dgate_ref, dup_ref, out_ref):
    slots, width = gate_ref.shape[1:]
    tokens, dwidth = dgate_ref.shape
    quarter = tokens // 4
    out_ref[...] = jnp.zeros_like(out_ref)
    activated, _ = silu_parts(gate_ref[0].astype(jnp.float32))
    hidden = activated * up_ref[0].astype(jnp.float32)
    pad = jnp.zeros((SLOT_ROWS - slots, width), jnp.float32)
    out_ref[:SLOT_ROWS, :width] = jnp.concatenate([hidden, pad], axis=0).astype(jnp.bfloat16)
    dactivated, _ = silu_parts(dgate_ref[...].astype(jnp.float32))
    dhidden = (dactivated * dup_ref[...].astype(jnp.float32)).astype(jnp.bfloat16)
    for j in range(4):
        out_ref[SLOT_ROWS : SLOT_ROWS + quarter, j * LANES : j * LANES + dwidth] = dhidden[
            j * quarter : (j + 1) * quarter
        ]


def pick_kernel(capacity, nx, ny, expert_ref, part_ref, rows_ref, prob_ref, ids_ref, slots_ref, out_ref, cols_ref):
    expert, part = expert_ref[0], part_ref[0]
    eighth = out_ref.shape[0]
    tokens, width = rows_ref.shape
    lane = lax.broadcasted_iota(jnp.int32, (eighth, tokens), 1)
    row = lax.broadcasted_iota(jnp.int32, (eighth, tokens), 0)
    chosen = jnp.where(lane == row + part * eighth, 1.0, 0.0).astype(jnp.bfloat16)
    token = expert * tokens + lax.broadcasted_iota(jnp.int32, (2, tokens), 1)
    meta = jnp.concatenate(
        [
            ids_ref[...].astype(jnp.float32),
            (slots_ref[...] + expert * capacity).astype(jnp.float32),
            prob_ref[...].astype(jnp.float32),
            token.astype(jnp.float32),
        ],
        axis=0,
    ).astype(jnp.bfloat16)
    meta = jnp.concatenate([meta, jnp.zeros((LANES - 8, tokens), jnp.bfloat16)], axis=0)
    meta = dot(chosen, meta, ((1,), (1,))).astype(jnp.bfloat16)
    picked = dot(chosen, rows_ref[...], ((1,), (0,))).astype(jnp.bfloat16)
    out_ref[:, :width] = picked
    out_ref[:, width:] = meta
    block = width // (nx * ny)
    stride = cols_ref.shape[2] // nx
    for y in range(ny):
        for x in range(nx):
            at = (x * ny + y) * block
            cols_ref[y, :, x * stride : x * stride + block] = picked[:, at : at + block]
            cols_ref[y, :, x * stride + block : (x + 1) * stride] = meta[:, : stride - block]


def pack_kernel(cols_ref, rows_ref, out_ref):
    ny, _, span = cols_ref.shape
    for y in range(ny):
        out_ref[:, y * span : (y + 1) * span] = cols_ref[y]
    out_ref[:, ny * span :] = rows_ref[...]


def routing(meta, expert):
    hit0 = meta[:, 0:1] == expert
    hit1 = meta[:, 1:2] == expert
    slot = jnp.where(hit0, meta[:, 2:3], jnp.where(hit1, meta[:, 3:4], -1.0)).astype(jnp.int32)
    prob = jnp.where(hit0, meta[:, 4:5], jnp.where(hit1, meta[:, 5:6], 0.0))
    token = meta[:, 6:7].astype(jnp.int32)
    return slot, prob, token


def one_hot(index, count, value=1.0):
    lane = lax.broadcasted_iota(jnp.int32, (index.shape[0], count), 1)
    return jnp.where(lane == index, value, 0.0).astype(jnp.bfloat16)


def dot(a, b, dims):
    return lax.dot_general(a, b, (dims, ((), ())), preferred_element_type=jnp.float32)


def weight_kernel(block, ny, expert_ref, *refs):
    pieces, hid_ref, out_ref, a_ref, be_ref, bd_ref = refs[:6], *refs[6:11]
    rows, total = pieces[0].shape
    span = total // ny
    group = 6 * rows
    expert = expert_ref[0].astype(jnp.float32)
    width = be_ref.shape[1]
    quarter = hid_ref.shape[1] - SLOT_ROWS
    for y in range(ny):
        top = y * group
        for i, piece in enumerate(pieces):
            a_ref[top + i * rows : top + (i + 1) * rows, :] = piece[:, y * span : (y + 1) * span]
        at = y * span + block
        meta = jnp.concatenate([piece[:, at : at + 8] for piece in pieces], axis=0)
        slot, prob, token = routing(meta.astype(jnp.float32), expert)
        weighted = dot(one_hot(slot, SLOT_ROWS, prob), hid_ref[y, :SLOT_ROWS, :width], ((1,), (0,)))
        be_ref[top : top + group, :] = weighted.astype(jnp.bfloat16)
        dense = jnp.concatenate(
            [hid_ref[y, SLOT_ROWS:, j * LANES : (j + 1) * LANES] for j in range(4)], axis=0
        )
        moved = dot(one_hot(token, 4 * quarter), dense, ((1,), (0,)))
        bd_ref[top : top + group, :] = moved.astype(jnp.bfloat16)
    rows_in = a_ref[...]
    nx, height, stride = out_ref.shape
    summed = dot(be_ref[...], rows_in, ((0,), (0,))).astype(jnp.bfloat16)
    dsummed = dot(bd_ref[...], rows_in, ((0,), (0,))).astype(jnp.bfloat16)
    for x in range(nx):
        out_ref[x, :width, :] = summed[:, x * stride : (x + 1) * stride]
        out_ref[x, width:, :] = dsummed[: height - width, x * stride : (x + 1) * stride]


def sum_kernel(scale, in_ref, dots_ref, expert_ref, dense_ref, dots_out):
    dots_out[...] = jnp.sum(dots_ref[...], axis=0)
    summed = in_ref[0].astype(jnp.float32)
    for x in range(1, in_ref.shape[0]):
        summed = summed + in_ref[x].astype(jnp.float32)
    summed = (summed * scale).astype(jnp.bfloat16)
    width, block = expert_ref.shape
    expert_ref[...] = summed[:width, :block]
    dense_ref[...] = summed[width : width + dense_ref.shape[0], :block]


def place(onehot, values):
    high = values.astype(jnp.bfloat16)
    rest = values - high.astype(jnp.float32)
    middle = rest.astype(jnp.bfloat16)
    low = (rest - middle.astype(jnp.float32)).astype(jnp.bfloat16)
    dims = ((0,), (0,))
    return dot(onehot, high, dims) + dot(onehot, middle, dims) + dot(onehot, low, dims)


def back_kernel(expert_ref, *refs):
    datas, metas = refs[:6], refs[6:12]
    we_ref, wd_ref, gate_ref, up_ref, dgate_ref, dup_ref = refs[12:18]
    gate_out, up_out, dots_out, dgate_out, dup_out = refs[18:23]
    acc_e, acc_d = refs[23:25]
    step = pl.program_id(0)

    @pl.when(step == 0)
    def _():
        acc_e[...] = jnp.zeros_like(acc_e)
        acc_d[...] = jnp.zeros_like(acc_d)

    rows = jnp.concatenate([data[...] for data in datas], axis=0)
    acc_e[...] += dot(rows, we_ref[0], ((1,), (1,)))
    acc_d[...] += dot(rows, wd_ref[...], ((1,), (1,)))

    @pl.when(step == pl.num_programs(0) - 1)
    def _():
        meta = jnp.concatenate([m[...] for m in metas], axis=0).astype(jnp.float32)
        slot, prob, token = routing(meta, expert_ref[0].astype(jnp.float32))
        slots = gate_ref.shape[1]
        hot = one_hot(slot, slots)
        back = place(hot, acc_e[...])
        wide = jnp.broadcast_to(prob, (prob.shape[0], LANES)).astype(jnp.bfloat16)
        slot_prob = dot(hot, wide, ((0,), (0,)))[:, :1]
        up_val = up_ref[0].astype(jnp.float32)
        activated, slope = silu_parts(gate_ref[0].astype(jnp.float32))
        product = back * (activated * up_val)
        ones = jnp.ones((8, product.shape[1]), jnp.float32)
        dots_out[...] = lax.dot_general(
            ones,
            product,
            (((1,), (1,)), ((), ())),
            precision=lax.Precision.HIGHEST,
            preferred_element_type=jnp.float32,
        )[:1]
        scaled = slot_prob * back
        gate_out[0] = (scaled * up_val * slope).astype(jnp.bfloat16)
        up_out[0] = (scaled * activated).astype(jnp.bfloat16)
        dback = place(one_hot(token, dgate_ref.shape[0]), acc_d[...])
        dactivated, dslope = silu_parts(dgate_ref[...].astype(jnp.float32))
        dgate_out[...] = (dback * dup_ref[...].astype(jnp.float32) * dslope).astype(jnp.bfloat16)
        dup_out[...] = (dback * dactivated).astype(jnp.bfloat16)


def ring(count, step):
    return [(i, (i + step) % count) for i in range(count)]


def local(
    grad_out,
    gate_prob,
    expert_ids,
    slot_positions,
    expert_down,
    dense_down,
    expert_gate_pre,
    expert_up_pre,
    dense_gate_pre,
    dense_up_pre,
):
    nx, ny, ne = lax.axis_size("x"), lax.axis_size("y"), lax.axis_size("e")
    expert, part = lax.axis_index("e"), lax.axis_index(("l", "c"))
    tokens, width = grad_out.shape
    slots, hwidth = expert_gate_pre.shape[1:]
    dwidth = dense_gate_pre.shape[1]
    capacity = slots // ne
    eighth = tokens // (RUN * CORES)
    block = width // (nx * ny)
    bf16 = jnp.bfloat16
    stride = -(-(block + 8) // LANES) * LANES
    expert_arr = expert.reshape(1).astype(jnp.int32)
    smem = pl.BlockSpec(memory_space=pltpu.SMEM)
    vmem = pl.BlockSpec(memory_space=pltpu.VMEM)

    hidden = pl.pallas_call(
        hidden_kernel,
        out_shape=jax.ShapeDtypeStruct((SLOT_ROWS + ne * tokens // 4, 4 * LANES), bf16),
        compiler_params=params(),
    )(expert_gate_pre, expert_up_pre, dense_gate_pre, dense_up_pre)
    hiddens = lax.all_gather(hidden, "y", axis=0)

    part_arr = part.reshape(1).astype(jnp.int32)
    span = nx * stride
    mine, cols = pl.pallas_call(
        functools.partial(pick_kernel, capacity, nx, ny),
        out_shape=(
            jax.ShapeDtypeStruct((eighth, width + LANES), bf16),
            jax.ShapeDtypeStruct((ny, eighth, span), bf16),
        ),
        in_specs=[smem] * 2 + [vmem] * 4,
        compiler_params=params(),
    )(expert_arr, part_arr, grad_out, gate_prob.T, expert_ids.T, slot_positions.T)
    cols = lax.all_to_all(cols, "y", split_axis=0, concat_axis=0, tiled=True)
    packed = pl.pallas_call(
        pack_kernel,
        out_shape=jax.ShapeDtypeStruct((eighth, ny * span + width + LANES), bf16),
        compiler_params=params(),
    )(cols, mine)
    packed = lax.all_gather(packed, "e", axis=0, tiled=True)
    pieces = [packed] + [lax.ppermute(packed, ("e", "l"), ring(ne * RUN, d)) for d in (1, -1)]
    pieces += [lax.ppermute(p, "c", ring(CORES, 1)) for p in pieces]

    height = hwidth + -(-dwidth // 16) * 16
    ktotal = ny * ne * tokens
    partial_sums = pl.pallas_call(
        functools.partial(weight_kernel, block, ny),
        grid=(1,),
        out_shape=jax.ShapeDtypeStruct((nx, height, stride), bf16),
        in_specs=[smem]
        + [pl.BlockSpec((ne * eighth, ny * span), lambda k: (0, 0))] * 6
        + [whole(*hiddens.shape)],
        out_specs=whole(nx, height, stride),
        scratch_shapes=[
            pltpu.VMEM((ktotal, span), bf16),
            pltpu.VMEM((ktotal, hwidth), bf16),
            pltpu.VMEM((ktotal, LANES), bf16),
        ],
        compiler_params=params(),
    )(expert_arr, *pieces, hiddens)
    partial_sums, expert_arr = lax.optimization_barrier((partial_sums, expert_arr))
    landed = lax.all_to_all(partial_sums, "x", split_axis=0, concat_axis=0, tiled=True)

    depth = math.gcd(ny * span, width)
    base = ny * span // depth
    data_spec = pl.BlockSpec((ne * eighth, depth), lambda k: (0, base + k))
    meta_spec = pl.BlockSpec((ne * eighth, LANES), lambda k: (0, (ny * span + width) // LANES))
    gate_grad, up_grad, dots, dense_gate_grad, dense_up_grad = pl.pallas_call(
        back_kernel,
        grid=(width // depth,),
        out_shape=(
            jax.ShapeDtypeStruct((1, slots, hwidth), bf16),
            jax.ShapeDtypeStruct((1, slots, hwidth), bf16),
            jax.ShapeDtypeStruct((1, slots), jnp.float32),
            jax.ShapeDtypeStruct((ne * tokens, dwidth), bf16),
            jax.ShapeDtypeStruct((ne * tokens, dwidth), bf16),
        ),
        in_specs=[smem]
        + [data_spec] * 6
        + [meta_spec] * 6
        + [
            pl.BlockSpec((1, hwidth, depth), lambda k: (0, 0, k)),
            pl.BlockSpec((dwidth, depth), lambda k: (0, k)),
            whole(1, slots, hwidth),
            whole(1, slots, hwidth),
            whole(ne * tokens, dwidth),
            whole(ne * tokens, dwidth),
        ],
        out_specs=(
            whole(1, slots, hwidth),
            whole(1, slots, hwidth),
            whole(1, slots),
            whole(ne * tokens, dwidth),
            whole(ne * tokens, dwidth),
        ),
        scratch_shapes=[
            pltpu.VMEM((ne * tokens, hwidth), jnp.float32),
            pltpu.VMEM((ne * tokens, dwidth), jnp.float32),
        ],
        compiler_params=params(),
    )(
        expert_arr,
        *pieces,
        *pieces,
        expert_down,
        dense_down,
        expert_gate_pre,
        expert_up_pre,
        dense_gate_pre,
        dense_up_pre,
    )

    all_dots = lax.all_gather(dots, ("l", "c"), axis=0)
    expert_down_grad, dense_down_grad, slot_prob_grad = pl.pallas_call(
        functools.partial(sum_kernel, 1.0 / (nx * ny)),
        out_shape=(
            jax.ShapeDtypeStruct((hwidth, block), bf16),
            jax.ShapeDtypeStruct((dwidth, block), bf16),
            jax.ShapeDtypeStruct((1, slots), jnp.float32),
        ),
        compiler_params=params(),
    )(landed, all_dots)
    return (
        gate_grad,
        up_grad,
        slot_prob_grad,
        expert_down_grad.T[None],
        dense_gate_grad,
        dense_up_grad,
        dense_down_grad.T,
    )


def solution(mesh):
    n_dp, n_expert, n_tensor = (mesh.shape[a] for a in ("dp", "expert", "tensor"))
    fine = Mesh(
        mesh.devices.reshape(X_CHIPS, n_dp // X_CHIPS, n_expert, n_tensor // CORES, CORES),
        ("x", "y", "e", "l", "c"),
    )
    dp, tensor = ("x", "y"), ("l", "c")
    return jax.shard_map(
        local,
        mesh=fine,
        in_specs=(
            P((*dp, "e"), None),
            P((*dp, "e"), None),
            P((*dp, "e"), None),
            P((*dp, "e"), None),
            P("e", tensor, None),
            P(("e", *tensor), None),
            P("e", dp, tensor),
            P("e", dp, tensor),
            P(dp, ("e", *tensor)),
            P(dp, ("e", *tensor)),
        ),
        out_specs=(
            P("e", dp, tensor),
            P("e", dp, tensor),
            P("e", dp),
            P("e", dp, tensor),
            P(dp, ("e", *tensor)),
            P(dp, ("e", *tensor)),
            P(dp, ("e", *tensor)),
        ),
        check_vma=False,
    )
```

```python
import functools
import math

import jax
import jax.numpy as jnp
from jax import lax
from jax.experimental import pallas as pl
from jax.experimental.pallas import tpu as pltpu
from jax.sharding import Mesh
from jax.sharding import PartitionSpec as P

X_CHIPS = 4
RUN = 3
CORES = 2
LANES = 128
SLOT_ROWS = 160
VMEM_BYTES = 56 * 1024 * 1024


def silu_parts(gate_val):
    gate_sig = jax.nn.sigmoid(gate_val)
    activated = gate_val * gate_sig
    slope = gate_sig * (1.0 + gate_val * (1.0 - gate_sig))
    return (activated, slope)


def whole(*shape):
    return pl.BlockSpec(shape, lambda *idx: (0,) * len(shape))


def params():
    return pltpu.CompilerParams(vmem_limit_bytes=VMEM_BYTES)


def hidden_kernel(gate_ref, up_ref, dgate_ref, dup_ref, out_ref):
    slots, width = gate_ref.shape[1:]
    tokens, dwidth = dgate_ref.shape
    quarter = tokens // 4
    out_ref[...] = jnp.zeros_like(out_ref)
    activated, _ = silu_parts(gate_ref[0].astype(jnp.float32))
    hidden = activated * up_ref[0].astype(jnp.float32)
    pad = jnp.zeros((SLOT_ROWS - slots, width), jnp.float32)
    out_ref[:SLOT_ROWS, :width] = jnp.concatenate([hidden, pad], axis=0).astype(jnp.bfloat16)
    dactivated, _ = silu_parts(dgate_ref[...].astype(jnp.float32))
    dhidden = (dactivated * dup_ref[...].astype(jnp.float32)).astype(jnp.bfloat16)
    for j in range(4):
        out_ref[SLOT_ROWS : SLOT_ROWS + quarter, j * LANES : j * LANES + dwidth] = dhidden[
            j * quarter : (j + 1) * quarter
        ]


def pick_kernel(capacity, expert_ref, part_ref, rows_ref, prob_ref, ids_ref, slots_ref, out_ref):
    expert, part = expert_ref[0], part_ref[0]
    eighth = out_ref.shape[0]
    tokens, width = rows_ref.shape
    lane = lax.broadcasted_iota(jnp.int32, (eighth, tokens), 1)
    row = lax.broadcasted_iota(jnp.int32, (eighth, tokens), 0)
    chosen = jnp.where(lane == row + part * eighth, 1.0, 0.0).astype(jnp.bfloat16)
    out_ref[:, :width] = dot(chosen, rows_ref[...], ((1,), (0,))).astype(jnp.bfloat16)
    token = expert * tokens + lax.broadcasted_iota(jnp.int32, (2, tokens), 1)
    meta = jnp.concatenate(
        [
            ids_ref[...].astype(jnp.float32),
            (slots_ref[...] + expert * capacity).astype(jnp.float32),
            prob_ref[...].astype(jnp.float32),
            token.astype(jnp.float32),
        ],
        axis=0,
    ).astype(jnp.bfloat16)
    meta = jnp.concatenate([meta, jnp.zeros((LANES - 8, tokens), jnp.bfloat16)], axis=0)
    out_ref[:, width:] = dot(chosen, meta, ((1,), (1,))).astype(jnp.bfloat16)


def split_kernel(nx, ny, rows_ref, out_ref):
    width = rows_ref.shape[1] - LANES
    block = width // (nx * ny)
    stride = out_ref.shape[2] // nx
    for y in range(ny):
        for x in range(nx):
            at = (x * ny + y) * block
            out_ref[y, :, x * stride : x * stride + block] = rows_ref[:, at : at + block]
            out_ref[y, :, x * stride + block : (x + 1) * stride] = rows_ref[
                :, width : width + stride - block
            ]


def routing(meta, expert):
    hit0 = meta[:, 0:1] == expert
    hit1 = meta[:, 1:2] == expert
    slot = jnp.where(hit0, meta[:, 2:3], jnp.where(hit1, meta[:, 3:4], -1.0)).astype(jnp.int32)
    prob = jnp.where(hit0, meta[:, 4:5], jnp.where(hit1, meta[:, 5:6], 0.0))
    token = meta[:, 6:7].astype(jnp.int32)
    return slot, prob, token


def one_hot(index, count, value=1.0):
    lane = lax.broadcasted_iota(jnp.int32, (index.shape[0], count), 1)
    return jnp.where(lane == index, value, 0.0).astype(jnp.bfloat16)


def dot(a, b, dims):
    return lax.dot_general(a, b, (dims, ((), ())), preferred_element_type=jnp.float32)


def weight_kernel(block, expert_ref, *refs):
    pieces, hid_ref, out_ref, a_ref, be_ref, bd_ref = refs[:6], *refs[6:11]
    ny, rows, _ = pieces[0].shape
    group = 6 * rows
    expert = expert_ref[0].astype(jnp.float32)
    width = be_ref.shape[1]
    quarter = hid_ref.shape[1] - SLOT_ROWS
    for y in range(ny):
        top = y * group
        for i, piece in enumerate(pieces):
            a_ref[top + i * rows : top + (i + 1) * rows, :] = piece[y]
        meta = jnp.concatenate([piece[y, :, block : block + 8] for piece in pieces], axis=0)
        slot, prob, token = routing(meta.astype(jnp.float32), expert)
        weighted = dot(one_hot(slot, SLOT_ROWS, prob), hid_ref[y, :SLOT_ROWS, :width], ((1,), (0,)))
        be_ref[top : top + group, :] = weighted.astype(jnp.bfloat16)
        dense = jnp.concatenate(
            [hid_ref[y, SLOT_ROWS:, j * LANES : (j + 1) * LANES] for j in range(4)], axis=0
        )
        moved = dot(one_hot(token, 4 * quarter), dense, ((1,), (0,)))
        bd_ref[top : top + group, :] = moved.astype(jnp.bfloat16)
    rows_in = a_ref[...]
    nx, height, stride = out_ref.shape
    summed = dot(be_ref[...], rows_in, ((0,), (0,))).astype(jnp.bfloat16)
    dsummed = dot(bd_ref[...], rows_in, ((0,), (0,))).astype(jnp.bfloat16)
    for x in range(nx):
        out_ref[x, :width, :] = summed[:, x * stride : (x + 1) * stride]
        out_ref[x, width:, :] = dsummed[: height - width, x * stride : (x + 1) * stride]


def sum_kernel(scale, in_ref, dots_ref, expert_ref, dense_ref, dots_out):
    dots_out[...] = jnp.sum(dots_ref[...], axis=0)
    summed = in_ref[0].astype(jnp.float32)
    for x in range(1, in_ref.shape[0]):
        summed = summed + in_ref[x].astype(jnp.float32)
    summed = (summed * scale).astype(jnp.bfloat16)
    width, block = expert_ref.shape
    expert_ref[...] = summed[:width, :block]
    dense_ref[...] = summed[width : width + dense_ref.shape[0], :block]


def place(onehot, values):
    high = values.astype(jnp.bfloat16)
    rest = values - high.astype(jnp.float32)
    middle = rest.astype(jnp.bfloat16)
    low = (rest - middle.astype(jnp.float32)).astype(jnp.bfloat16)
    dims = ((0,), (0,))
    return dot(onehot, high, dims) + dot(onehot, middle, dims) + dot(onehot, low, dims)


def back_kernel(expert_ref, *refs):
    datas, metas = refs[:6], refs[6:12]
    we_ref, wd_ref, gate_ref, up_ref, dgate_ref, dup_ref = refs[12:18]
    gate_out, up_out, dots_out, dgate_out, dup_out = refs[18:23]
    acc_e, acc_d = refs[23:25]
    step = pl.program_id(0)

    @pl.when(step == 0)
    def _():
        acc_e[...] = jnp.zeros_like(acc_e)
        acc_d[...] = jnp.zeros_like(acc_d)

    rows = jnp.concatenate([data[...] for data in datas], axis=0)
    acc_e[...] += dot(rows, we_ref[0], ((1,), (1,)))
    acc_d[...] += dot(rows, wd_ref[...], ((1,), (1,)))

    @pl.when(step == pl.num_programs(0) - 1)
    def _():
        meta = jnp.concatenate([m[...] for m in metas], axis=0).astype(jnp.float32)
        slot, prob, token = routing(meta, expert_ref[0].astype(jnp.float32))
        slots = gate_ref.shape[1]
        hot = one_hot(slot, slots)
        back = place(hot, acc_e[...])
        wide = jnp.broadcast_to(prob, (prob.shape[0], LANES)).astype(jnp.bfloat16)
        slot_prob = dot(hot, wide, ((0,), (0,)))[:, :1]
        up_val = up_ref[0].astype(jnp.float32)
        activated, slope = silu_parts(gate_ref[0].astype(jnp.float32))
        product = back * (activated * up_val)
        ones = jnp.ones((8, product.shape[1]), jnp.float32)
        dots_out[...] = lax.dot_general(
            ones,
            product,
            (((1,), (1,)), ((), ())),
            precision=lax.Precision.HIGHEST,
            preferred_element_type=jnp.float32,
        )[:1]
        scaled = slot_prob * back
        gate_out[0] = (scaled * up_val * slope).astype(jnp.bfloat16)
        up_out[0] = (scaled * activated).astype(jnp.bfloat16)
        dback = place(one_hot(token, dgate_ref.shape[0]), acc_d[...])
        dactivated, dslope = silu_parts(dgate_ref[...].astype(jnp.float32))
        dgate_out[...] = (dback * dup_ref[...].astype(jnp.float32) * dslope).astype(jnp.bfloat16)
        dup_out[...] = (dback * dactivated).astype(jnp.bfloat16)


def ring(count, step):
    return [(i, (i + step) % count) for i in range(count)]


def local(
    grad_out,
    gate_prob,
    expert_ids,
    slot_positions,
    expert_down,
    dense_down,
    expert_gate_pre,
    expert_up_pre,
    dense_gate_pre,
    dense_up_pre,
):
    nx, ny, ne = lax.axis_size("x"), lax.axis_size("y"), lax.axis_size("e")
    expert, part = lax.axis_index("e"), lax.axis_index(("l", "c"))
    tokens, width = grad_out.shape
    slots, hwidth = expert_gate_pre.shape[1:]
    dwidth = dense_gate_pre.shape[1]
    capacity = slots // ne
    eighth = tokens // (RUN * CORES)
    block = width // (nx * ny)
    bf16 = jnp.bfloat16
    stride = -(-(block + 8) // LANES) * LANES
    expert_arr = expert.reshape(1).astype(jnp.int32)
    smem = pl.BlockSpec(memory_space=pltpu.SMEM)
    vmem = pl.BlockSpec(memory_space=pltpu.VMEM)

    hidden = pl.pallas_call(
        hidden_kernel,
        out_shape=jax.ShapeDtypeStruct((SLOT_ROWS + ne * tokens // 4, 4 * LANES), bf16),
        compiler_params=params(),
    )(expert_gate_pre, expert_up_pre, dense_gate_pre, dense_up_pre)
    hiddens = lax.all_gather(hidden, "y", axis=0)

    part_arr = part.reshape(1).astype(jnp.int32)
    mine = pl.pallas_call(
        functools.partial(pick_kernel, capacity),
        out_shape=jax.ShapeDtypeStruct((eighth, width + LANES), bf16),
        in_specs=[smem] * 2 + [vmem] * 4,
        compiler_params=params(),
    )(expert_arr, part_arr, grad_out, gate_prob.T, expert_ids.T, slot_positions.T)
    rows = lax.all_gather(mine, "e", axis=0, tiled=True)

    chunks = pl.pallas_call(
        functools.partial(split_kernel, nx, ny),
        out_shape=jax.ShapeDtypeStruct((ny, ne * eighth, nx * stride), bf16),
        compiler_params=params(),
    )(rows)
    rows, chunks = lax.optimization_barrier((rows, chunks))
    chunks = lax.all_to_all(chunks, "y", split_axis=0, concat_axis=0, tiled=True)

    def spread(piece):
        along = [piece] + [lax.ppermute(piece, ("e", "l"), ring(ne * RUN, d)) for d in (1, -1)]
        other = [lax.ppermute(p, "c", ring(CORES, 1)) for p in along]
        return along + other

    row_pieces = spread(rows)
    chunks, *row_pieces = lax.optimization_barrier((chunks, *row_pieces))
    chunk_pieces = spread(chunks)

    height = hwidth + -(-dwidth // 16) * 16
    ktotal = ny * ne * tokens
    partial_sums = pl.pallas_call(
        functools.partial(weight_kernel, block),
        out_shape=jax.ShapeDtypeStruct((nx, height, stride), bf16),
        in_specs=[smem] + [vmem] * 7,
        scratch_shapes=[
            pltpu.VMEM((ktotal, nx * stride), bf16),
            pltpu.VMEM((ktotal, hwidth), bf16),
            pltpu.VMEM((ktotal, LANES), bf16),
        ],
        compiler_params=params(),
    )(expert_arr, *chunk_pieces, hiddens)
    partial_sums, expert_arr = lax.optimization_barrier((partial_sums, expert_arr))
    landed = lax.all_to_all(partial_sums, "x", split_axis=0, concat_axis=0, tiled=True)

    depth = math.gcd(1024, width)
    data_spec = pl.BlockSpec((ne * eighth, depth), lambda k: (0, k))
    meta_spec = pl.BlockSpec((ne * eighth, LANES), lambda k: (0, width // LANES))
    gate_grad, up_grad, dots, dense_gate_grad, dense_up_grad = pl.pallas_call(
        back_kernel,
        grid=(width // depth,),
        out_shape=(
            jax.ShapeDtypeStruct((1, slots, hwidth), bf16),
            jax.ShapeDtypeStruct((1, slots, hwidth), bf16),
            jax.ShapeDtypeStruct((1, slots), jnp.float32),
            jax.ShapeDtypeStruct((ne * tokens, dwidth), bf16),
            jax.ShapeDtypeStruct((ne * tokens, dwidth), bf16),
        ),
        in_specs=[smem]
        + [data_spec] * 6
        + [meta_spec] * 6
        + [
            pl.BlockSpec((1, hwidth, depth), lambda k: (0, 0, k)),
            pl.BlockSpec((dwidth, depth), lambda k: (0, k)),
            whole(1, slots, hwidth),
            whole(1, slots, hwidth),
            whole(ne * tokens, dwidth),
            whole(ne * tokens, dwidth),
        ],
        out_specs=(
            whole(1, slots, hwidth),
            whole(1, slots, hwidth),
            whole(1, slots),
            whole(ne * tokens, dwidth),
            whole(ne * tokens, dwidth),
        ),
        scratch_shapes=[
            pltpu.VMEM((ne * tokens, hwidth), jnp.float32),
            pltpu.VMEM((ne * tokens, dwidth), jnp.float32),
        ],
        compiler_params=params(),
    )(
        expert_arr,
        *row_pieces,
        *row_pieces,
        expert_down,
        dense_down,
        expert_gate_pre,
        expert_up_pre,
        dense_gate_pre,
        dense_up_pre,
    )

    all_dots = lax.all_gather(dots, ("l", "c"), axis=0)
    expert_down_grad, dense_down_grad, slot_prob_grad = pl.pallas_call(
        functools.partial(sum_kernel, 1.0 / (nx * ny)),
        out_shape=(
            jax.ShapeDtypeStruct((hwidth, block), bf16),
            jax.ShapeDtypeStruct((dwidth, block), bf16),
            jax.ShapeDtypeStruct((1, slots), jnp.float32),
        ),
        compiler_params=params(),
    )(landed, all_dots)
    return (
        gate_grad,
        up_grad,
        slot_prob_grad,
        expert_down_grad.T[None],
        dense_gate_grad,
        dense_up_grad,
        dense_down_grad.T,
    )


def solution(mesh):
    n_dp, n_expert, n_tensor = (mesh.shape[a] for a in ("dp", "expert", "tensor"))
    fine = Mesh(
        mesh.devices.reshape(X_CHIPS, n_dp // X_CHIPS, n_expert, n_tensor // CORES, CORES),
        ("x", "y", "e", "l", "c"),
    )
    dp, tensor = ("x", "y"), ("l", "c")
    return jax.shard_map(
        local,
        mesh=fine,
        in_specs=(
            P((*dp, "e"), None),
            P((*dp, "e"), None),
            P((*dp, "e"), None),
            P((*dp, "e"), None),
            P("e", tensor, None),
            P(("e", *tensor), None),
            P("e", dp, tensor),
            P("e", dp, tensor),
            P(dp, ("e", *tensor)),
            P(dp, ("e", *tensor)),
        ),
        out_specs=(
            P("e", dp, tensor),
            P("e", dp, tensor),
            P("e", dp),
            P("e", dp, tensor),
            P(dp, ("e", *tensor)),
            P(dp, ("e", *tensor)),
            P(dp, ("e", *tensor)),
        ),
        check_vma=False,
    )
```

```python
import functools
import math

import jax
import jax.numpy as jnp
from jax import lax
from jax.experimental import pallas as pl
from jax.experimental.pallas import tpu as pltpu
from jax.sharding import Mesh
from jax.sharding import PartitionSpec as P

X_CHIPS = 4
RUN = 3
CORES = 2
LANES = 128
SLOT_ROWS = 160
VMEM_BYTES = 56 * 1024 * 1024


def silu_parts(gate_val):
    gate_sig = jax.nn.sigmoid(gate_val)
    activated = gate_val * gate_sig
    slope = gate_sig * (1.0 + gate_val * (1.0 - gate_sig))
    return (activated, slope)


def whole(*shape):
    return pl.BlockSpec(shape, lambda *idx: (0,) * len(shape))


def params():
    return pltpu.CompilerParams(vmem_limit_bytes=VMEM_BYTES)


def hidden_kernel(gate_ref, up_ref, dgate_ref, dup_ref, out_ref):
    slots, width = gate_ref.shape[1:]
    tokens, dwidth = dgate_ref.shape
    quarter = tokens // 4
    out_ref[...] = jnp.zeros_like(out_ref)
    activated, _ = silu_parts(gate_ref[0].astype(jnp.float32))
    hidden = activated * up_ref[0].astype(jnp.float32)
    pad = jnp.zeros((SLOT_ROWS - slots, width), jnp.float32)
    out_ref[:SLOT_ROWS, :width] = jnp.concatenate([hidden, pad], axis=0).astype(jnp.bfloat16)
    dactivated, _ = silu_parts(dgate_ref[...].astype(jnp.float32))
    dhidden = (dactivated * dup_ref[...].astype(jnp.float32)).astype(jnp.bfloat16)
    for j in range(4):
        out_ref[SLOT_ROWS : SLOT_ROWS + quarter, j * LANES : j * LANES + dwidth] = dhidden[
            j * quarter : (j + 1) * quarter
        ]


def pick_kernel(capacity, nx, ny, expert_ref, part_ref, rows_ref, prob_ref, ids_ref, slots_ref, out_ref, cols_ref):
    expert, part = expert_ref[0], part_ref[0]
    eighth = out_ref.shape[0]
    tokens, width = rows_ref.shape
    lane = lax.broadcasted_iota(jnp.int32, (eighth, tokens), 1)
    row = lax.broadcasted_iota(jnp.int32, (eighth, tokens), 0)
    chosen = jnp.where(lane == row + part * eighth, 1.0, 0.0).astype(jnp.bfloat16)
    token = expert * tokens + lax.broadcasted_iota(jnp.int32, (2, tokens), 1)
    meta = jnp.concatenate(
        [
            ids_ref[...].astype(jnp.float32),
            (slots_ref[...] + expert * capacity).astype(jnp.float32),
            prob_ref[...].astype(jnp.float32),
            token.astype(jnp.float32),
        ],
        axis=0,
    ).astype(jnp.bfloat16)
    meta = jnp.concatenate([meta, jnp.zeros((LANES - 8, tokens), jnp.bfloat16)], axis=0)
    meta = dot(chosen, meta, ((1,), (1,))).astype(jnp.bfloat16)
    picked = dot(chosen, rows_ref[...], ((1,), (0,))).astype(jnp.bfloat16)
    out_ref[:, :width] = picked
    out_ref[:, width:] = meta
    block = width // (nx * ny)
    stride = cols_ref.shape[2] // nx
    for y in range(ny):
        for x in range(nx):
            at = (x * ny + y) * block
            cols_ref[y, :, x * stride : x * stride + block] = picked[:, at : at + block]
            cols_ref[y, :, x * stride + block : (x + 1) * stride] = meta[:, : stride - block]


def routing(meta, expert):
    hit0 = meta[:, 0:1] == expert
    hit1 = meta[:, 1:2] == expert
    slot = jnp.where(hit0, meta[:, 2:3], jnp.where(hit1, meta[:, 3:4], -1.0)).astype(jnp.int32)
    prob = jnp.where(hit0, meta[:, 4:5], jnp.where(hit1, meta[:, 5:6], 0.0))
    token = meta[:, 6:7].astype(jnp.int32)
    return slot, prob, token


def one_hot(index, count, value=1.0):
    lane = lax.broadcasted_iota(jnp.int32, (index.shape[0], count), 1)
    return jnp.where(lane == index, value, 0.0).astype(jnp.bfloat16)


def dot(a, b, dims):
    return lax.dot_general(a, b, (dims, ((), ())), preferred_element_type=jnp.float32)


def weight_kernel(block, ny, expert_ref, *refs):
    pieces, hid_ref, out_ref, a_ref, be_ref, bd_ref = refs[:6], *refs[6:11]
    rows, total = pieces[0].shape
    span = total // ny
    group = 6 * rows
    expert = expert_ref[0].astype(jnp.float32)
    width = be_ref.shape[1]
    quarter = hid_ref.shape[1] - SLOT_ROWS
    for y in range(ny):
        top = y * group
        for i, piece in enumerate(pieces):
            a_ref[top + i * rows : top + (i + 1) * rows, :] = piece[:, y * span : (y + 1) * span]
        at = y * span + block
        meta = jnp.concatenate([piece[:, at : at + 8] for piece in pieces], axis=0)
        slot, prob, token = routing(meta.astype(jnp.float32), expert)
        weighted = dot(one_hot(slot, SLOT_ROWS, prob), hid_ref[y, :SLOT_ROWS, :width], ((1,), (0,)))
        be_ref[top : top + group, :] = weighted.astype(jnp.bfloat16)
        dense = jnp.concatenate(
            [hid_ref[y, SLOT_ROWS:, j * LANES : (j + 1) * LANES] for j in range(4)], axis=0
        )
        moved = dot(one_hot(token, 4 * quarter), dense, ((1,), (0,)))
        bd_ref[top : top + group, :] = moved.astype(jnp.bfloat16)
    rows_in = a_ref[...]
    nx, height, stride = out_ref.shape
    summed = dot(be_ref[...], rows_in, ((0,), (0,))).astype(jnp.bfloat16)
    dsummed = dot(bd_ref[...], rows_in, ((0,), (0,))).astype(jnp.bfloat16)
    for x in range(nx):
        out_ref[x, :width, :] = summed[:, x * stride : (x + 1) * stride]
        out_ref[x, width:, :] = dsummed[: height - width, x * stride : (x + 1) * stride]


def sum_kernel(scale, in_ref, dots_ref, expert_ref, dense_ref, dots_out):
    dots_out[...] = jnp.sum(dots_ref[...], axis=0)
    summed = in_ref[0].astype(jnp.float32)
    for x in range(1, in_ref.shape[0]):
        summed = summed + in_ref[x].astype(jnp.float32)
    summed = (summed * scale).astype(jnp.bfloat16)
    width, block = expert_ref.shape
    expert_ref[...] = summed[:width, :block]
    dense_ref[...] = summed[width : width + dense_ref.shape[0], :block]


def place(onehot, values):
    high = values.astype(jnp.bfloat16)
    rest = values - high.astype(jnp.float32)
    middle = rest.astype(jnp.bfloat16)
    low = (rest - middle.astype(jnp.float32)).astype(jnp.bfloat16)
    dims = ((0,), (0,))
    return dot(onehot, high, dims) + dot(onehot, middle, dims) + dot(onehot, low, dims)


def back_kernel(expert_ref, *refs):
    datas, metas = refs[:6], refs[6:12]
    we_ref, wd_ref, gate_ref, up_ref, dgate_ref, dup_ref = refs[12:18]
    gate_out, up_out, dots_out, dgate_out, dup_out = refs[18:23]
    acc_e, acc_d = refs[23:25]
    step = pl.program_id(0)

    @pl.when(step == 0)
    def _():
        acc_e[...] = jnp.zeros_like(acc_e)
        acc_d[...] = jnp.zeros_like(acc_d)

    rows = jnp.concatenate([data[...] for data in datas], axis=0)
    acc_e[...] += dot(rows, we_ref[0], ((1,), (1,)))
    acc_d[...] += dot(rows, wd_ref[...], ((1,), (1,)))

    @pl.when(step == pl.num_programs(0) - 1)
    def _():
        meta = jnp.concatenate([m[...] for m in metas], axis=0).astype(jnp.float32)
        slot, prob, token = routing(meta, expert_ref[0].astype(jnp.float32))
        slots = gate_ref.shape[1]
        hot = one_hot(slot, slots)
        back = place(hot, acc_e[...])
        wide = jnp.broadcast_to(prob, (prob.shape[0], LANES)).astype(jnp.bfloat16)
        slot_prob = dot(hot, wide, ((0,), (0,)))[:, :1]
        up_val = up_ref[0].astype(jnp.float32)
        activated, slope = silu_parts(gate_ref[0].astype(jnp.float32))
        product = back * (activated * up_val)
        ones = jnp.ones((8, product.shape[1]), jnp.float32)
        dots_out[...] = lax.dot_general(
            ones,
            product,
            (((1,), (1,)), ((), ())),
            precision=lax.Precision.HIGHEST,
            preferred_element_type=jnp.float32,
        )[:1]
        scaled = slot_prob * back
        gate_out[0] = (scaled * up_val * slope).astype(jnp.bfloat16)
        up_out[0] = (scaled * activated).astype(jnp.bfloat16)
        dback = place(one_hot(token, dgate_ref.shape[0]), acc_d[...])
        dactivated, dslope = silu_parts(dgate_ref[...].astype(jnp.float32))
        dgate_out[...] = (dback * dup_ref[...].astype(jnp.float32) * dslope).astype(jnp.bfloat16)
        dup_out[...] = (dback * dactivated).astype(jnp.bfloat16)


def ring(count, step):
    return [(i, (i + step) % count) for i in range(count)]


def local(
    grad_out,
    gate_prob,
    expert_ids,
    slot_positions,
    expert_down,
    dense_down,
    expert_gate_pre,
    expert_up_pre,
    dense_gate_pre,
    dense_up_pre,
):
    nx, ny, ne = lax.axis_size("x"), lax.axis_size("y"), lax.axis_size("e")
    expert, part = lax.axis_index("e"), lax.axis_index(("l", "c"))
    tokens, width = grad_out.shape
    slots, hwidth = expert_gate_pre.shape[1:]
    dwidth = dense_gate_pre.shape[1]
    capacity = slots // ne
    eighth = tokens // (RUN * CORES)
    block = width // (nx * ny)
    bf16 = jnp.bfloat16
    stride = -(-(block + 8) // LANES) * LANES
    expert_arr = expert.reshape(1).astype(jnp.int32)
    smem = pl.BlockSpec(memory_space=pltpu.SMEM)
    vmem = pl.BlockSpec(memory_space=pltpu.VMEM)

    hidden = pl.pallas_call(
        hidden_kernel,
        out_shape=jax.ShapeDtypeStruct((SLOT_ROWS + ne * tokens // 4, 4 * LANES), bf16),
        compiler_params=params(),
    )(expert_gate_pre, expert_up_pre, dense_gate_pre, dense_up_pre)
    hiddens = lax.all_gather(hidden, "y", axis=0)

    part_arr = part.reshape(1).astype(jnp.int32)
    span = nx * stride
    mine, cols = pl.pallas_call(
        functools.partial(pick_kernel, capacity, nx, ny),
        out_shape=(
            jax.ShapeDtypeStruct((eighth, width + LANES), bf16),
            jax.ShapeDtypeStruct((ny, eighth, span), bf16),
        ),
        in_specs=[smem] * 2 + [vmem] * 4,
        compiler_params=params(),
    )(expert_arr, part_arr, grad_out, gate_prob.T, expert_ids.T, slot_positions.T)
    cols = lax.all_to_all(cols, "y", split_axis=0, concat_axis=0, tiled=True)
    rows = lax.all_gather(mine, "e", axis=0, tiled=True)
    cols, rows = lax.optimization_barrier((cols, rows))
    cols = lax.all_gather(
        cols.transpose(1, 0, 2).reshape(eighth, ny * span), "e", axis=0, tiled=True
    )
    cols, rows = lax.optimization_barrier((cols, rows))

    def along(piece):
        return [piece] + [lax.ppermute(piece, ("e", "l"), ring(ne * RUN, d)) for d in (1, -1)]

    def other(pieces):
        return pieces + [lax.ppermute(p, "c", ring(CORES, 1)) for p in pieces]

    chunk_pieces = other(along(cols))
    row_pieces = other(along(rows))

    height = hwidth + -(-dwidth // 16) * 16
    ktotal = ny * ne * tokens
    partial_sums = pl.pallas_call(
        functools.partial(weight_kernel, block, ny),
        out_shape=jax.ShapeDtypeStruct((nx, height, stride), bf16),
        in_specs=[smem] + [vmem] * 7,
        scratch_shapes=[
            pltpu.VMEM((ktotal, span), bf16),
            pltpu.VMEM((ktotal, hwidth), bf16),
            pltpu.VMEM((ktotal, LANES), bf16),
        ],
        compiler_params=params(),
    )(expert_arr, *chunk_pieces, hiddens)
    partial_sums, expert_arr = lax.optimization_barrier((partial_sums, expert_arr))
    landed = lax.all_to_all(partial_sums, "x", split_axis=0, concat_axis=0, tiled=True)

    depth = math.gcd(1024, width)
    data_spec = pl.BlockSpec((ne * eighth, depth), lambda k: (0, k))
    meta_spec = pl.BlockSpec((ne * eighth, LANES), lambda k: (0, width // LANES))
    gate_grad, up_grad, dots, dense_gate_grad, dense_up_grad = pl.pallas_call(
        back_kernel,
        grid=(width // depth,),
        out_shape=(
            jax.ShapeDtypeStruct((1, slots, hwidth), bf16),
            jax.ShapeDtypeStruct((1, slots, hwidth), bf16),
            jax.ShapeDtypeStruct((1, slots), jnp.float32),
            jax.ShapeDtypeStruct((ne * tokens, dwidth), bf16),
            jax.ShapeDtypeStruct((ne * tokens, dwidth), bf16),
        ),
        in_specs=[smem]
        + [data_spec] * 6
        + [meta_spec] * 6
        + [
            pl.BlockSpec((1, hwidth, depth), lambda k: (0, 0, k)),
            pl.BlockSpec((dwidth, depth), lambda k: (0, k)),
            whole(1, slots, hwidth),
            whole(1, slots, hwidth),
            whole(ne * tokens, dwidth),
            whole(ne * tokens, dwidth),
        ],
        out_specs=(
            whole(1, slots, hwidth),
            whole(1, slots, hwidth),
            whole(1, slots),
            whole(ne * tokens, dwidth),
            whole(ne * tokens, dwidth),
        ),
        scratch_shapes=[
            pltpu.VMEM((ne * tokens, hwidth), jnp.float32),
            pltpu.VMEM((ne * tokens, dwidth), jnp.float32),
        ],
        compiler_params=params(),
    )(
        expert_arr,
        *row_pieces,
        *row_pieces,
        expert_down,
        dense_down,
        expert_gate_pre,
        expert_up_pre,
        dense_gate_pre,
        dense_up_pre,
    )

    all_dots = lax.all_gather(dots, ("l", "c"), axis=0)
    expert_down_grad, dense_down_grad, slot_prob_grad = pl.pallas_call(
        functools.partial(sum_kernel, 1.0 / (nx * ny)),
        out_shape=(
            jax.ShapeDtypeStruct((hwidth, block), bf16),
            jax.ShapeDtypeStruct((dwidth, block), bf16),
            jax.ShapeDtypeStruct((1, slots), jnp.float32),
        ),
        compiler_params=params(),
    )(landed, all_dots)
    return (
        gate_grad,
        up_grad,
        slot_prob_grad,
        expert_down_grad.T[None],
        dense_gate_grad,
        dense_up_grad,
        dense_down_grad.T,
    )


def solution(mesh):
    n_dp, n_expert, n_tensor = (mesh.shape[a] for a in ("dp", "expert", "tensor"))
    fine = Mesh(
        mesh.devices.reshape(X_CHIPS, n_dp // X_CHIPS, n_expert, n_tensor // CORES, CORES),
        ("x", "y", "e", "l", "c"),
    )
    dp, tensor = ("x", "y"), ("l", "c")
    return jax.shard_map(
        local,
        mesh=fine,
        in_specs=(
            P((*dp, "e"), None),
            P((*dp, "e"), None),
            P((*dp, "e"), None),
            P((*dp, "e"), None),
            P("e", tensor, None),
            P(("e", *tensor), None),
            P("e", dp, tensor),
            P("e", dp, tensor),
            P(dp, ("e", *tensor)),
            P(dp, ("e", *tensor)),
        ),
        out_specs=(
            P("e", dp, tensor),
            P("e", dp, tensor),
            P("e", dp),
            P("e", dp, tensor),
            P(dp, ("e", *tensor)),
            P(dp, ("e", *tensor)),
            P(dp, ("e", *tensor)),
        ),
        check_vma=False,
    )
```

```python
import functools
import math

import jax
import jax.numpy as jnp
from jax import lax
from jax.experimental import pallas as pl
from jax.experimental.pallas import tpu as pltpu
from jax.sharding import Mesh
from jax.sharding import PartitionSpec as P

X_CHIPS = 4
RUN = 3
CORES = 2
LANES = 128
SLOT_ROWS = 160
VMEM_BYTES = 56 * 1024 * 1024


def silu_parts(gate_val):
    gate_sig = jax.nn.sigmoid(gate_val)
    activated = gate_val * gate_sig
    slope = gate_sig * (1.0 + gate_val * (1.0 - gate_sig))
    return (activated, slope)


def whole(*shape):
    return pl.BlockSpec(shape, lambda *idx: (0,) * len(shape))


def params():
    return pltpu.CompilerParams(vmem_limit_bytes=VMEM_BYTES)


def hidden_kernel(gate_ref, up_ref, dgate_ref, dup_ref, out_ref):
    slots, width = gate_ref.shape[1:]
    tokens, dwidth = dgate_ref.shape
    quarter = tokens // 4
    out_ref[...] = jnp.zeros_like(out_ref)
    activated, _ = silu_parts(gate_ref[0].astype(jnp.float32))
    hidden = activated * up_ref[0].astype(jnp.float32)
    pad = jnp.zeros((SLOT_ROWS - slots, width), jnp.float32)
    out_ref[:SLOT_ROWS, :width] = jnp.concatenate([hidden, pad], axis=0).astype(jnp.bfloat16)
    dactivated, _ = silu_parts(dgate_ref[...].astype(jnp.float32))
    dhidden = (dactivated * dup_ref[...].astype(jnp.float32)).astype(jnp.bfloat16)
    for j in range(4):
        out_ref[SLOT_ROWS : SLOT_ROWS + quarter, j * LANES : j * LANES + dwidth] = dhidden[
            j * quarter : (j + 1) * quarter
        ]


def pick_kernel(capacity, expert_ref, part_ref, rows_ref, prob_ref, ids_ref, slots_ref, out_ref):
    expert, part = expert_ref[0], part_ref[0]
    eighth = out_ref.shape[0]
    tokens, width = rows_ref.shape
    lane = lax.broadcasted_iota(jnp.int32, (eighth, tokens), 1)
    row = lax.broadcasted_iota(jnp.int32, (eighth, tokens), 0)
    chosen = jnp.where(lane == row + part * eighth, 1.0, 0.0).astype(jnp.bfloat16)
    out_ref[:, :width] = dot(chosen, rows_ref[...], ((1,), (0,))).astype(jnp.bfloat16)
    token = expert * tokens + lax.broadcasted_iota(jnp.int32, (2, tokens), 1)
    meta = jnp.concatenate(
        [
            ids_ref[...].astype(jnp.float32),
            (slots_ref[...] + expert * capacity).astype(jnp.float32),
            prob_ref[...].astype(jnp.float32),
            token.astype(jnp.float32),
        ],
        axis=0,
    ).astype(jnp.bfloat16)
    meta = jnp.concatenate([meta, jnp.zeros((LANES - 8, tokens), jnp.bfloat16)], axis=0)
    out_ref[:, width:] = dot(chosen, meta, ((1,), (1,))).astype(jnp.bfloat16)


def split_kernel(nx, ny, rows_ref, out_ref):
    width = rows_ref.shape[1] - LANES
    block = width // (nx * ny)
    stride = out_ref.shape[2] // nx
    for y in range(ny):
        for x in range(nx):
            at = (x * ny + y) * block
            out_ref[y, :, x * stride : x * stride + block] = rows_ref[:, at : at + block]
            out_ref[y, :, x * stride + block : (x + 1) * stride] = rows_ref[
                :, width : width + stride - block
            ]


def routing(meta, expert):
    hit0 = meta[:, 0:1] == expert
    hit1 = meta[:, 1:2] == expert
    slot = jnp.where(hit0, meta[:, 2:3], jnp.where(hit1, meta[:, 3:4], -1.0)).astype(jnp.int32)
    prob = jnp.where(hit0, meta[:, 4:5], jnp.where(hit1, meta[:, 5:6], 0.0))
    token = meta[:, 6:7].astype(jnp.int32)
    return slot, prob, token


def one_hot(index, count, value=1.0):
    lane = lax.broadcasted_iota(jnp.int32, (index.shape[0], count), 1)
    return jnp.where(lane == index, value, 0.0).astype(jnp.bfloat16)


def dot(a, b, dims):
    return lax.dot_general(a, b, (dims, ((), ())), preferred_element_type=jnp.float32)


def weight_kernel(block, expert_ref, *refs):
    pieces, hid_ref, out_ref, a_ref, be_ref, bd_ref = refs[:6], *refs[6:11]
    ny, rows, _ = pieces[0].shape
    group = 6 * rows
    expert = expert_ref[0].astype(jnp.float32)
    width = be_ref.shape[1]
    quarter = hid_ref.shape[1] - SLOT_ROWS
    for y in range(ny):
        top = y * group
        for i, piece in enumerate(pieces):
            a_ref[top + i * rows : top + (i + 1) * rows, :] = piece[y]
        meta = jnp.concatenate([piece[y, :, block : block + 8] for piece in pieces], axis=0)
        slot, prob, token = routing(meta.astype(jnp.float32), expert)
        weighted = dot(one_hot(slot, SLOT_ROWS, prob), hid_ref[y, :SLOT_ROWS, :width], ((1,), (0,)))
        be_ref[top : top + group, :] = weighted.astype(jnp.bfloat16)
        dense = jnp.concatenate(
            [hid_ref[y, SLOT_ROWS:, j * LANES : (j + 1) * LANES] for j in range(4)], axis=0
        )
        moved = dot(one_hot(token, 4 * quarter), dense, ((1,), (0,)))
        bd_ref[top : top + group, :] = moved.astype(jnp.bfloat16)
    rows_in = a_ref[...]
    nx, height, stride = out_ref.shape
    summed = dot(be_ref[...], rows_in, ((0,), (0,))).astype(jnp.bfloat16)
    dsummed = dot(bd_ref[...], rows_in, ((0,), (0,))).astype(jnp.bfloat16)
    for x in range(nx):
        out_ref[x, :width, :] = summed[:, x * stride : (x + 1) * stride]
        out_ref[x, width:, :] = dsummed[: height - width, x * stride : (x + 1) * stride]


def place(onehot, values):
    high = values.astype(jnp.bfloat16)
    rest = values - high.astype(jnp.float32)
    middle = rest.astype(jnp.bfloat16)
    low = (rest - middle.astype(jnp.float32)).astype(jnp.bfloat16)
    dims = ((0,), (0,))
    return dot(onehot, high, dims) + dot(onehot, middle, dims) + dot(onehot, low, dims)


def product_kernel(*refs):
    datas, we_ref, wd_ref, acc_e, acc_d = refs[:6], *refs[6:10]

    @pl.when(pl.program_id(0) == 0)
    def _():
        acc_e[...] = jnp.zeros_like(acc_e)
        acc_d[...] = jnp.zeros_like(acc_d)

    rows = jnp.concatenate([data[...] for data in datas], axis=0)
    acc_e[...] += dot(rows, we_ref[0], ((1,), (1,)))
    acc_d[...] += dot(rows, wd_ref[...], ((1,), (1,)))


def back_kernel(expert_ref, *refs):
    metas = refs[:6]
    acc_e, acc_d, gate_ref, up_ref, dgate_ref, dup_ref = refs[6:12]
    gate_out, up_out, dots_out, dgate_out, dup_out = refs[12:17]
    meta = jnp.concatenate([m[...] for m in metas], axis=0).astype(jnp.float32)
    slot, prob, token = routing(meta, expert_ref[0].astype(jnp.float32))
    slots = gate_ref.shape[1]
    hot = one_hot(slot, slots)
    back = place(hot, acc_e[...])
    wide = jnp.broadcast_to(prob, (prob.shape[0], LANES)).astype(jnp.bfloat16)
    slot_prob = dot(hot, wide, ((0,), (0,)))[:, :1]
    up_val = up_ref[0].astype(jnp.float32)
    activated, slope = silu_parts(gate_ref[0].astype(jnp.float32))
    product = back * (activated * up_val)
    ones = jnp.ones((8, product.shape[1]), jnp.float32)
    dots_out[...] = lax.dot_general(
        ones,
        product,
        (((1,), (1,)), ((), ())),
        precision=lax.Precision.HIGHEST,
        preferred_element_type=jnp.float32,
    )[:1]
    scaled = slot_prob * back
    gate_out[0] = (scaled * up_val * slope).astype(jnp.bfloat16)
    up_out[0] = (scaled * activated).astype(jnp.bfloat16)
    dback = place(one_hot(token, dgate_ref.shape[0]), acc_d[...])
    dactivated, dslope = silu_parts(dgate_ref[...].astype(jnp.float32))
    dgate_out[...] = (dback * dup_ref[...].astype(jnp.float32) * dslope).astype(jnp.bfloat16)
    dup_out[...] = (dback * dactivated).astype(jnp.bfloat16)


def ring(count, step):
    return [(i, (i + step) % count) for i in range(count)]


def local(
    grad_out,
    gate_prob,
    expert_ids,
    slot_positions,
    expert_down,
    dense_down,
    expert_gate_pre,
    expert_up_pre,
    dense_gate_pre,
    dense_up_pre,
):
    nx, ny, ne = lax.axis_size("x"), lax.axis_size("y"), lax.axis_size("e")
    expert, part = lax.axis_index("e"), lax.axis_index(("l", "c"))
    tokens, width = grad_out.shape
    slots, hwidth = expert_gate_pre.shape[1:]
    dwidth = dense_gate_pre.shape[1]
    capacity = slots // ne
    eighth = tokens // (RUN * CORES)
    block = width // (nx * ny)
    bf16 = jnp.bfloat16
    stride = -(-(block + 8) // LANES) * LANES
    expert_arr = expert.reshape(1).astype(jnp.int32)
    smem = pl.BlockSpec(memory_space=pltpu.SMEM)
    vmem = pl.BlockSpec(memory_space=pltpu.VMEM)

    hidden = pl.pallas_call(
        hidden_kernel,
        out_shape=jax.ShapeDtypeStruct((SLOT_ROWS + ne * tokens // 4, 4 * LANES), bf16),
        compiler_params=params(),
    )(expert_gate_pre, expert_up_pre, dense_gate_pre, dense_up_pre)
    hiddens = lax.all_gather(hidden, "y", axis=0)

    part_arr = part.reshape(1).astype(jnp.int32)
    mine = pl.pallas_call(
        functools.partial(pick_kernel, capacity),
        out_shape=jax.ShapeDtypeStruct((eighth, width + LANES), bf16),
        in_specs=[smem] * 2 + [vmem] * 4,
        compiler_params=params(),
    )(expert_arr, part_arr, grad_out, gate_prob.T, expert_ids.T, slot_positions.T)
    rows = lax.all_gather(mine, "e", axis=0, tiled=True)

    chunks = pl.pallas_call(
        functools.partial(split_kernel, nx, ny),
        out_shape=jax.ShapeDtypeStruct((ny, ne * eighth, nx * stride), bf16),
        compiler_params=params(),
    )(rows)
    rows, chunks = lax.optimization_barrier((rows, chunks))
    chunks = lax.all_to_all(chunks, "y", split_axis=0, concat_axis=0, tiled=True)

    def along(piece):
        return [piece] + [lax.ppermute(piece, ("e", "l"), ring(ne * RUN, d)) for d in (1, -1)]

    def other(pieces):
        return pieces + [lax.ppermute(p, "c", ring(CORES, 1)) for p in pieces]

    row_pieces = other(along(rows))
    chunks, *row_pieces = lax.optimization_barrier((chunks, *row_pieces))

    depth = math.gcd(1024, width)
    acc_e, acc_d = pl.pallas_call(
        product_kernel,
        grid=(width // depth,),
        out_shape=(
            jax.ShapeDtypeStruct((ne * tokens, hwidth), jnp.float32),
            jax.ShapeDtypeStruct((ne * tokens, dwidth), jnp.float32),
        ),
        in_specs=[pl.BlockSpec((ne * eighth, depth), lambda k: (0, k))] * 6
        + [
            pl.BlockSpec((1, hwidth, depth), lambda k: (0, 0, k)),
            pl.BlockSpec((dwidth, depth), lambda k: (0, k)),
        ],
        out_specs=(whole(ne * tokens, hwidth), whole(ne * tokens, dwidth)),
        compiler_params=params(),
    )(*row_pieces, expert_down, dense_down)

    near, up, down = along(chunks)
    up, down, acc_e, acc_d = lax.optimization_barrier((up, down, acc_e, acc_d))
    chunk_pieces = other([near, up, down])

    height = hwidth + -(-dwidth // 16) * 16
    ktotal = ny * ne * tokens
    partial_sums = pl.pallas_call(
        functools.partial(weight_kernel, block),
        out_shape=jax.ShapeDtypeStruct((nx, height, stride), bf16),
        in_specs=[smem] + [vmem] * 7,
        scratch_shapes=[
            pltpu.VMEM((ktotal, nx * stride), bf16),
            pltpu.VMEM((ktotal, hwidth), bf16),
            pltpu.VMEM((ktotal, LANES), bf16),
        ],
        compiler_params=params(),
    )(expert_arr, *chunk_pieces, hiddens)
    partial_sums, expert_arr = lax.optimization_barrier((partial_sums, expert_arr))
    landed = lax.all_to_all(partial_sums, "x", split_axis=0, concat_axis=0, tiled=True)

    meta_spec = pl.BlockSpec((ne * eighth, LANES), lambda k: (0, width // LANES))
    gate_grad, up_grad, dots, dense_gate_grad, dense_up_grad = pl.pallas_call(
        back_kernel,
        grid=(1,),
        out_shape=(
            jax.ShapeDtypeStruct((1, slots, hwidth), bf16),
            jax.ShapeDtypeStruct((1, slots, hwidth), bf16),
            jax.ShapeDtypeStruct((1, slots), jnp.float32),
            jax.ShapeDtypeStruct((ne * tokens, dwidth), bf16),
            jax.ShapeDtypeStruct((ne * tokens, dwidth), bf16),
        ),
        in_specs=[smem]
        + [meta_spec] * 6
        + [
            whole(ne * tokens, hwidth),
            whole(ne * tokens, dwidth),
            whole(1, slots, hwidth),
            whole(1, slots, hwidth),
            whole(ne * tokens, dwidth),
            whole(ne * tokens, dwidth),
        ],
        out_specs=(
            whole(1, slots, hwidth),
            whole(1, slots, hwidth),
            whole(1, slots),
            whole(ne * tokens, dwidth),
            whole(ne * tokens, dwidth),
        ),
        compiler_params=params(),
    )(
        expert_arr,
        *row_pieces,
        acc_e,
        acc_d,
        expert_gate_pre,
        expert_up_pre,
        dense_gate_pre,
        dense_up_pre,
    )
    all_dots = lax.all_gather(dots, ("l", "c"), axis=0)

    def total(top, count):
        parts = [landed[x, top : top + count, :block].astype(jnp.float32) for x in range(nx)]
        return (sum(parts[1:], parts[0]) * (1.0 / (nx * ny))).astype(bf16)

    expert_down_grad = total(0, hwidth)
    dense_down_grad = total(hwidth, dwidth)
    slot_prob_grad = jnp.sum(all_dots, axis=0)
    return (
        gate_grad,
        up_grad,
        slot_prob_grad,
        expert_down_grad.T[None],
        dense_gate_grad,
        dense_up_grad,
        dense_down_grad.T,
    )


def solution(mesh):
    n_dp, n_expert, n_tensor = (mesh.shape[a] for a in ("dp", "expert", "tensor"))
    fine = Mesh(
        mesh.devices.reshape(X_CHIPS, n_dp // X_CHIPS, n_expert, n_tensor // CORES, CORES),
        ("x", "y", "e", "l", "c"),
    )
    dp, tensor = ("x", "y"), ("l", "c")
    return jax.shard_map(
        local,
        mesh=fine,
        in_specs=(
            P((*dp, "e"), None),
            P((*dp, "e"), None),
            P((*dp, "e"), None),
            P((*dp, "e"), None),
            P("e", tensor, None),
            P(("e", *tensor), None),
            P("e", dp, tensor),
            P("e", dp, tensor),
            P(dp, ("e", *tensor)),
            P(dp, ("e", *tensor)),
        ),
        out_specs=(
            P("e", dp, tensor),
            P("e", dp, tensor),
            P("e", dp),
            P("e", dp, tensor),
            P(dp, ("e", *tensor)),
            P(dp, ("e", *tensor)),
            P(dp, ("e", *tensor)),
        ),
        check_vma=False,
    )
```

```python
import functools
import math

import jax
import jax.numpy as jnp
from jax import lax
from jax.experimental import pallas as pl
from jax.experimental.pallas import tpu as pltpu
from jax.sharding import Mesh
from jax.sharding import PartitionSpec as P

X_CHIPS = 4
RUN = 3
CORES = 2
LANES = 128
SLOT_ROWS = 160
VMEM_BYTES = 56 * 1024 * 1024


def silu_parts(gate_val):
    gate_sig = jax.nn.sigmoid(gate_val)
    activated = gate_val * gate_sig
    slope = gate_sig * (1.0 + gate_val * (1.0 - gate_sig))
    return (activated, slope)


def whole(*shape):
    return pl.BlockSpec(shape, lambda *idx: (0,) * len(shape))


def params():
    return pltpu.CompilerParams(vmem_limit_bytes=VMEM_BYTES)


def hidden_kernel(gate_ref, up_ref, dgate_ref, dup_ref, out_ref):
    slots, width = gate_ref.shape[1:]
    tokens, dwidth = dgate_ref.shape
    quarter = tokens // 4
    out_ref[0] = jnp.zeros_like(out_ref[0])
    activated, _ = silu_parts(gate_ref[0].astype(jnp.float32))
    hidden = activated * up_ref[0].astype(jnp.float32)
    pad = jnp.zeros((SLOT_ROWS - slots, width), jnp.float32)
    out_ref[0, :SLOT_ROWS, :width] = jnp.concatenate([hidden, pad], axis=0).astype(jnp.bfloat16)
    dactivated, _ = silu_parts(dgate_ref[...].astype(jnp.float32))
    dhidden = (dactivated * dup_ref[...].astype(jnp.float32)).astype(jnp.bfloat16)
    for j in range(4):
        out_ref[0, SLOT_ROWS : SLOT_ROWS + quarter, j * LANES : j * LANES + dwidth] = dhidden[
            j * quarter : (j + 1) * quarter
        ]
    for y in range(1, out_ref.shape[0]):
        out_ref[y] = out_ref[0]


def pick_kernel(capacity, expert_ref, part_ref, rows_ref, prob_ref, ids_ref, slots_ref, out_ref):
    expert, part = expert_ref[0], part_ref[0]
    eighth = out_ref.shape[0]
    tokens, width = rows_ref.shape
    lane = lax.broadcasted_iota(jnp.int32, (eighth, tokens), 1)
    row = lax.broadcasted_iota(jnp.int32, (eighth, tokens), 0)
    chosen = jnp.where(lane == row + part * eighth, 1.0, 0.0).astype(jnp.bfloat16)
    out_ref[:, :width] = dot(chosen, rows_ref[...], ((1,), (0,))).astype(jnp.bfloat16)
    token = expert * tokens + lax.broadcasted_iota(jnp.int32, (2, tokens), 1)
    meta = jnp.concatenate(
        [
            ids_ref[...].astype(jnp.float32),
            (slots_ref[...] + expert * capacity).astype(jnp.float32),
            prob_ref[...].astype(jnp.float32),
            token.astype(jnp.float32),
        ],
        axis=0,
    ).astype(jnp.bfloat16)
    meta = jnp.concatenate([meta, jnp.zeros((LANES - 8, tokens), jnp.bfloat16)], axis=0)
    out_ref[:, width:] = dot(chosen, meta, ((1,), (1,))).astype(jnp.bfloat16)


def split_kernel(nx, ny, rows_ref, out_ref):
    width = rows_ref.shape[1] - LANES
    block = width // (nx * ny)
    stride = out_ref.shape[2] // nx
    for y in range(ny):
        for x in range(nx):
            at = (x * ny + y) * block
            out_ref[y, :, x * stride : x * stride + block] = rows_ref[:, at : at + block]
            out_ref[y, :, x * stride + block : (x + 1) * stride] = rows_ref[
                :, width : width + stride - block
            ]


def routing(meta, expert):
    hit0 = meta[:, 0:1] == expert
    hit1 = meta[:, 1:2] == expert
    slot = jnp.where(hit0, meta[:, 2:3], jnp.where(hit1, meta[:, 3:4], -1.0)).astype(jnp.int32)
    prob = jnp.where(hit0, meta[:, 4:5], jnp.where(hit1, meta[:, 5:6], 0.0))
    token = meta[:, 6:7].astype(jnp.int32)
    return slot, prob, token


def one_hot(index, count, value=1.0):
    lane = lax.broadcasted_iota(jnp.int32, (index.shape[0], count), 1)
    return jnp.where(lane == index, value, 0.0).astype(jnp.bfloat16)


def dot(a, b, dims):
    return lax.dot_general(a, b, (dims, ((), ())), preferred_element_type=jnp.float32)


def weight_kernel(block, expert_ref, *refs):
    pieces, hid_ref, out_ref, a_ref, be_ref, bd_ref = refs[:6], *refs[6:11]
    ny, rows, _ = pieces[0].shape
    group = 6 * rows
    expert = expert_ref[0].astype(jnp.float32)
    width = be_ref.shape[1]
    quarter = hid_ref.shape[1] - SLOT_ROWS
    for y in range(ny):
        top = y * group
        for i, piece in enumerate(pieces):
            a_ref[top + i * rows : top + (i + 1) * rows, :] = piece[y]
        meta = jnp.concatenate([piece[y, :, block : block + 8] for piece in pieces], axis=0)
        slot, prob, token = routing(meta.astype(jnp.float32), expert)
        weighted = dot(one_hot(slot, SLOT_ROWS, prob), hid_ref[y, :SLOT_ROWS, :width], ((1,), (0,)))
        be_ref[top : top + group, :] = weighted.astype(jnp.bfloat16)
        dense = jnp.concatenate(
            [hid_ref[y, SLOT_ROWS:, j * LANES : (j + 1) * LANES] for j in range(4)], axis=0
        )
        moved = dot(one_hot(token, 4 * quarter), dense, ((1,), (0,)))
        bd_ref[top : top + group, :] = moved.astype(jnp.bfloat16)
    rows_in = a_ref[...]
    nx, height, stride = out_ref.shape
    summed = dot(be_ref[...], rows_in, ((0,), (0,))).astype(jnp.bfloat16)
    dsummed = dot(bd_ref[...], rows_in, ((0,), (0,))).astype(jnp.bfloat16)
    for x in range(nx):
        out_ref[x, :width, :] = summed[:, x * stride : (x + 1) * stride]
        out_ref[x, width:, :] = dsummed[: height - width, x * stride : (x + 1) * stride]


def place(onehot, values):
    high = values.astype(jnp.bfloat16)
    rest = values - high.astype(jnp.float32)
    middle = rest.astype(jnp.bfloat16)
    low = (rest - middle.astype(jnp.float32)).astype(jnp.bfloat16)
    dims = ((0,), (0,))
    return dot(onehot, high, dims) + dot(onehot, middle, dims) + dot(onehot, low, dims)


def product_kernel(*refs):
    datas, we_ref, wd_ref, acc_e, acc_d = refs[:6], *refs[6:10]

    @pl.when(pl.program_id(0) == 0)
    def _():
        acc_e[...] = jnp.zeros_like(acc_e)
        acc_d[...] = jnp.zeros_like(acc_d)

    rows = jnp.concatenate([data[...] for data in datas], axis=0)
    acc_e[...] += dot(rows, we_ref[0], ((1,), (1,)))
    acc_d[...] += dot(rows, wd_ref[...], ((1,), (1,)))


def back_kernel(expert_ref, *refs):
    metas = refs[:6]
    acc_e, acc_d, gate_ref, up_ref, dgate_ref, dup_ref = refs[6:12]
    gate_out, up_out, dots_out, dgate_out, dup_out = refs[12:17]
    meta = jnp.concatenate([m[...] for m in metas], axis=0).astype(jnp.float32)
    slot, prob, token = routing(meta, expert_ref[0].astype(jnp.float32))
    slots = gate_ref.shape[1]
    hot = one_hot(slot, slots)
    back = place(hot, acc_e[...])
    wide = jnp.broadcast_to(prob, (prob.shape[0], LANES)).astype(jnp.bfloat16)
    slot_prob = dot(hot, wide, ((0,), (0,)))[:, :1]
    up_val = up_ref[0].astype(jnp.float32)
    activated, slope = silu_parts(gate_ref[0].astype(jnp.float32))
    product = back * (activated * up_val)
    ones = jnp.ones((8, product.shape[1]), jnp.float32)
    dots_out[...] = lax.dot_general(
        ones,
        product,
        (((1,), (1,)), ((), ())),
        precision=lax.Precision.HIGHEST,
        preferred_element_type=jnp.float32,
    )[:1]
    scaled = slot_prob * back
    gate_out[0] = (scaled * up_val * slope).astype(jnp.bfloat16)
    up_out[0] = (scaled * activated).astype(jnp.bfloat16)
    dback = place(one_hot(token, dgate_ref.shape[0]), acc_d[...])
    dactivated, dslope = silu_parts(dgate_ref[...].astype(jnp.float32))
    dgate_out[...] = (dback * dup_ref[...].astype(jnp.float32) * dslope).astype(jnp.bfloat16)
    dup_out[...] = (dback * dactivated).astype(jnp.bfloat16)


def ring(count, step):
    return [(i, (i + step) % count) for i in range(count)]


def local(
    grad_out,
    gate_prob,
    expert_ids,
    slot_positions,
    expert_down,
    dense_down,
    expert_gate_pre,
    expert_up_pre,
    dense_gate_pre,
    dense_up_pre,
):
    nx, ny, ne = lax.axis_size("x"), lax.axis_size("y"), lax.axis_size("e")
    expert, part = lax.axis_index("e"), lax.axis_index(("l", "c"))
    tokens, width = grad_out.shape
    slots, hwidth = expert_gate_pre.shape[1:]
    dwidth = dense_gate_pre.shape[1]
    capacity = slots // ne
    eighth = tokens // (RUN * CORES)
    block = width // (nx * ny)
    bf16 = jnp.bfloat16
    stride = -(-(block + 8) // LANES) * LANES
    expert_arr = expert.reshape(1).astype(jnp.int32)
    smem = pl.BlockSpec(memory_space=pltpu.SMEM)
    vmem = pl.BlockSpec(memory_space=pltpu.VMEM)

    hidden = pl.pallas_call(
        hidden_kernel,
        out_shape=jax.ShapeDtypeStruct((ny, SLOT_ROWS + ne * tokens // 4, 4 * LANES), bf16),
        compiler_params=params(),
    )(expert_gate_pre, expert_up_pre, dense_gate_pre, dense_up_pre)
    hiddens = lax.all_to_all(hidden, "y", split_axis=0, concat_axis=0, tiled=True)

    part_arr = part.reshape(1).astype(jnp.int32)
    mine = pl.pallas_call(
        functools.partial(pick_kernel, capacity),
        out_shape=jax.ShapeDtypeStruct((eighth, width + LANES), bf16),
        in_specs=[smem] * 2 + [vmem] * 4,
        compiler_params=params(),
    )(expert_arr, part_arr, grad_out, gate_prob.T, expert_ids.T, slot_positions.T)
    rows = lax.all_gather(mine, "e", axis=0, tiled=True)

    chunks = pl.pallas_call(
        functools.partial(split_kernel, nx, ny),
        out_shape=jax.ShapeDtypeStruct((ny, ne * eighth, nx * stride), bf16),
        compiler_params=params(),
    )(rows)
    rows, chunks = lax.optimization_barrier((rows, chunks))
    chunks, hiddens = lax.optimization_barrier((chunks, hiddens))
    chunks = lax.all_to_all(chunks, "y", split_axis=0, concat_axis=0, tiled=True)

    def along(piece):
        return [piece] + [lax.ppermute(piece, ("e", "l"), ring(ne * RUN, d)) for d in (1, -1)]

    def other(pieces):
        return pieces + [lax.ppermute(p, "c", ring(CORES, 1)) for p in pieces]

    row_pieces = other(along(rows))
    chunks, *row_pieces = lax.optimization_barrier((chunks, *row_pieces))

    depth = math.gcd(1024, width)
    acc_e, acc_d = pl.pallas_call(
        product_kernel,
        grid=(width // depth,),
        out_shape=(
            jax.ShapeDtypeStruct((ne * tokens, hwidth), jnp.float32),
            jax.ShapeDtypeStruct((ne * tokens, dwidth), jnp.float32),
        ),
        in_specs=[pl.BlockSpec((ne * eighth, depth), lambda k: (0, k))] * 6
        + [
            pl.BlockSpec((1, hwidth, depth), lambda k: (0, 0, k)),
            pl.BlockSpec((dwidth, depth), lambda k: (0, k)),
        ],
        out_specs=(whole(ne * tokens, hwidth), whole(ne * tokens, dwidth)),
        compiler_params=params(),
    )(*row_pieces, expert_down, dense_down)

    near, up, down = along(chunks)
    up, down, acc_e, acc_d = lax.optimization_barrier((up, down, acc_e, acc_d))
    chunk_pieces = other([near, up, down])

    height = hwidth + -(-dwidth // 16) * 16
    ktotal = ny * ne * tokens
    partial_sums = pl.pallas_call(
        functools.partial(weight_kernel, block),
        out_shape=jax.ShapeDtypeStruct((nx, height, stride), bf16),
        in_specs=[smem] + [vmem] * 7,
        scratch_shapes=[
            pltpu.VMEM((ktotal, nx * stride), bf16),
            pltpu.VMEM((ktotal, hwidth), bf16),
            pltpu.VMEM((ktotal, LANES), bf16),
        ],
        compiler_params=params(),
    )(expert_arr, *chunk_pieces, hiddens)
    partial_sums, expert_arr = lax.optimization_barrier((partial_sums, expert_arr))
    landed = lax.all_to_all(partial_sums, "x", split_axis=0, concat_axis=0, tiled=True)

    meta_spec = pl.BlockSpec((ne * eighth, LANES), lambda k: (0, width // LANES))
    gate_grad, up_grad, dots, dense_gate_grad, dense_up_grad = pl.pallas_call(
        back_kernel,
        grid=(1,),
        out_shape=(
            jax.ShapeDtypeStruct((1, slots, hwidth), bf16),
            jax.ShapeDtypeStruct((1, slots, hwidth), bf16),
            jax.ShapeDtypeStruct((1, slots), jnp.float32),
            jax.ShapeDtypeStruct((ne * tokens, dwidth), bf16),
            jax.ShapeDtypeStruct((ne * tokens, dwidth), bf16),
        ),
        in_specs=[smem]
        + [meta_spec] * 6
        + [
            whole(ne * tokens, hwidth),
            whole(ne * tokens, dwidth),
            whole(1, slots, hwidth),
            whole(1, slots, hwidth),
            whole(ne * tokens, dwidth),
            whole(ne * tokens, dwidth),
        ],
        out_specs=(
            whole(1, slots, hwidth),
            whole(1, slots, hwidth),
            whole(1, slots),
            whole(ne * tokens, dwidth),
            whole(ne * tokens, dwidth),
        ),
        compiler_params=params(),
    )(
        expert_arr,
        *row_pieces,
        acc_e,
        acc_d,
        expert_gate_pre,
        expert_up_pre,
        dense_gate_pre,
        dense_up_pre,
    )
    all_dots = lax.all_gather(dots, ("l", "c"), axis=0)

    def total(top, count):
        parts = [landed[x, top : top + count, :block].astype(jnp.float32) for x in range(nx)]
        return (sum(parts[1:], parts[0]) * (1.0 / (nx * ny))).astype(bf16)

    expert_down_grad = total(0, hwidth)
    dense_down_grad = total(hwidth, dwidth)
    slot_prob_grad = jnp.sum(all_dots, axis=0)
    return (
        gate_grad,
        up_grad,
        slot_prob_grad,
        expert_down_grad.T[None],
        dense_gate_grad,
        dense_up_grad,
        dense_down_grad.T,
    )


def solution(mesh):
    n_dp, n_expert, n_tensor = (mesh.shape[a] for a in ("dp", "expert", "tensor"))
    fine = Mesh(
        mesh.devices.reshape(X_CHIPS, n_dp // X_CHIPS, n_expert, n_tensor // CORES, CORES),
        ("x", "y", "e", "l", "c"),
    )
    dp, tensor = ("x", "y"), ("l", "c")
    return jax.shard_map(
        local,
        mesh=fine,
        in_specs=(
            P((*dp, "e"), None),
            P((*dp, "e"), None),
            P((*dp, "e"), None),
            P((*dp, "e"), None),
            P("e", tensor, None),
            P(("e", *tensor), None),
            P("e", dp, tensor),
            P("e", dp, tensor),
            P(dp, ("e", *tensor)),
            P(dp, ("e", *tensor)),
        ),
        out_specs=(
            P("e", dp, tensor),
            P("e", dp, tensor),
            P("e", dp),
            P("e", dp, tensor),
            P(dp, ("e", *tensor)),
            P(dp, ("e", *tensor)),
            P(dp, ("e", *tensor)),
        ),
        check_vma=False,
    )
```

```python
import functools
import math

import jax
import jax.numpy as jnp
from jax import lax
from jax.experimental import pallas as pl
from jax.experimental.pallas import tpu as pltpu
from jax.sharding import Mesh
from jax.sharding import PartitionSpec as P

X_CHIPS = 4
RUN = 3
CORES = 2
LANES = 128
SLOT_ROWS = 160
VMEM_BYTES = 56 * 1024 * 1024


def silu_parts(gate_val):
    gate_sig = jax.nn.sigmoid(gate_val)
    activated = gate_val * gate_sig
    slope = gate_sig * (1.0 + gate_val * (1.0 - gate_sig))
    return (activated, slope)


def whole(*shape):
    return pl.BlockSpec(shape, lambda *idx: (0,) * len(shape))


def params():
    return pltpu.CompilerParams(vmem_limit_bytes=VMEM_BYTES)


def hidden_kernel(gate_ref, up_ref, dgate_ref, dup_ref, out_ref):
    slots, width = gate_ref.shape[1:]
    tokens, dwidth = dgate_ref.shape
    quarter = tokens // 4
    out_ref[0] = jnp.zeros_like(out_ref[0])
    activated, _ = silu_parts(gate_ref[0].astype(jnp.float32))
    hidden = activated * up_ref[0].astype(jnp.float32)
    pad = jnp.zeros((SLOT_ROWS - slots, width), jnp.float32)
    out_ref[0, :SLOT_ROWS, :width] = jnp.concatenate([hidden, pad], axis=0).astype(jnp.bfloat16)
    dactivated, _ = silu_parts(dgate_ref[...].astype(jnp.float32))
    dhidden = (dactivated * dup_ref[...].astype(jnp.float32)).astype(jnp.bfloat16)
    for j in range(4):
        out_ref[0, SLOT_ROWS : SLOT_ROWS + quarter, j * LANES : j * LANES + dwidth] = dhidden[
            j * quarter : (j + 1) * quarter
        ]
    for y in range(1, out_ref.shape[0]):
        out_ref[y] = out_ref[0]


def pick_kernel(capacity, nx, ny, expert_ref, part_ref, rows_ref, prob_ref, ids_ref, slots_ref, out_ref, cols_ref):
    expert, part = expert_ref[0], part_ref[0]
    eighth = out_ref.shape[0]
    tokens, width = rows_ref.shape
    lane = lax.broadcasted_iota(jnp.int32, (eighth, tokens), 1)
    row = lax.broadcasted_iota(jnp.int32, (eighth, tokens), 0)
    chosen = jnp.where(lane == row + part * eighth, 1.0, 0.0).astype(jnp.bfloat16)
    token = expert * tokens + lax.broadcasted_iota(jnp.int32, (2, tokens), 1)
    meta = jnp.concatenate(
        [
            ids_ref[...].astype(jnp.float32),
            (slots_ref[...] + expert * capacity).astype(jnp.float32),
            prob_ref[...].astype(jnp.float32),
            token.astype(jnp.float32),
        ],
        axis=0,
    ).astype(jnp.bfloat16)
    meta = jnp.concatenate([meta, jnp.zeros((LANES - 8, tokens), jnp.bfloat16)], axis=0)
    meta = dot(chosen, meta, ((1,), (1,))).astype(jnp.bfloat16)
    picked = dot(chosen, rows_ref[...], ((1,), (0,))).astype(jnp.bfloat16)
    out_ref[:, :width] = picked
    out_ref[:, width:] = meta
    block = width // (nx * ny)
    stride = cols_ref.shape[2] // nx
    for y in range(ny):
        for x in range(nx):
            at = (x * ny + y) * block
            cols_ref[y, :, x * stride : x * stride + block] = picked[:, at : at + block]
            cols_ref[y, :, x * stride + block : (x + 1) * stride] = meta[:, : stride - block]


def pack_kernel(cols_ref, rows_ref, out_ref):
    ny, _, span = cols_ref.shape
    for y in range(ny):
        out_ref[:, y * span : (y + 1) * span] = cols_ref[y]
    out_ref[:, ny * span :] = rows_ref[...]


def routing(meta, expert):
    hit0 = meta[:, 0:1] == expert
    hit1 = meta[:, 1:2] == expert
    slot = jnp.where(hit0, meta[:, 2:3], jnp.where(hit1, meta[:, 3:4], -1.0)).astype(jnp.int32)
    prob = jnp.where(hit0, meta[:, 4:5], jnp.where(hit1, meta[:, 5:6], 0.0))
    token = meta[:, 6:7].astype(jnp.int32)
    return slot, prob, token


def one_hot(index, count, value=1.0):
    lane = lax.broadcasted_iota(jnp.int32, (index.shape[0], count), 1)
    return jnp.where(lane == index, value, 0.0).astype(jnp.bfloat16)


def dot(a, b, dims):
    return lax.dot_general(a, b, (dims, ((), ())), preferred_element_type=jnp.float32)


def weight_kernel(block, ny, expert_ref, *refs):
    pieces, hid_ref, out_ref, a_ref, be_ref, bd_ref = refs[:6], *refs[6:11]
    rows, total = pieces[0].shape
    span = total // ny
    group = 6 * rows
    expert = expert_ref[0].astype(jnp.float32)
    width = be_ref.shape[1]
    quarter = hid_ref.shape[1] - SLOT_ROWS
    for y in range(ny):
        top = y * group
        for i, piece in enumerate(pieces):
            a_ref[top + i * rows : top + (i + 1) * rows, :] = piece[:, y * span : (y + 1) * span]
        at = y * span + block
        meta = jnp.concatenate([piece[:, at : at + 8] for piece in pieces], axis=0)
        slot, prob, token = routing(meta.astype(jnp.float32), expert)
        weighted = dot(one_hot(slot, SLOT_ROWS, prob), hid_ref[y, :SLOT_ROWS, :width], ((1,), (0,)))
        be_ref[top : top + group, :] = weighted.astype(jnp.bfloat16)
        dense = jnp.concatenate(
            [hid_ref[y, SLOT_ROWS:, j * LANES : (j + 1) * LANES] for j in range(4)], axis=0
        )
        moved = dot(one_hot(token, 4 * quarter), dense, ((1,), (0,)))
        bd_ref[top : top + group, :] = moved.astype(jnp.bfloat16)
    rows_in = a_ref[...]
    nx, height, stride = out_ref.shape
    summed = dot(be_ref[...], rows_in, ((0,), (0,))).astype(jnp.bfloat16)
    dsummed = dot(bd_ref[...], rows_in, ((0,), (0,))).astype(jnp.bfloat16)
    for x in range(nx):
        out_ref[x, :width, :] = summed[:, x * stride : (x + 1) * stride]
        out_ref[x, width:, :] = dsummed[: height - width, x * stride : (x + 1) * stride]


def place(onehot, values):
    high = values.astype(jnp.bfloat16)
    rest = values - high.astype(jnp.float32)
    middle = rest.astype(jnp.bfloat16)
    low = (rest - middle.astype(jnp.float32)).astype(jnp.bfloat16)
    dims = ((0,), (0,))
    return dot(onehot, high, dims) + dot(onehot, middle, dims) + dot(onehot, low, dims)


def back_kernel(expert_ref, *refs):
    datas, metas = refs[:6], refs[6:12]
    we_ref, wd_ref, gate_ref, up_ref, dgate_ref, dup_ref = refs[12:18]
    gate_out, up_out, dots_out, dgate_out, dup_out = refs[18:23]
    acc_e, acc_d = refs[23:25]
    step = pl.program_id(0)

    @pl.when(step == 0)
    def _():
        acc_e[...] = jnp.zeros_like(acc_e)
        acc_d[...] = jnp.zeros_like(acc_d)

    rows = jnp.concatenate([data[...] for data in datas], axis=0)
    acc_e[...] += dot(rows, we_ref[0], ((1,), (1,)))
    acc_d[...] += dot(rows, wd_ref[...], ((1,), (1,)))

    @pl.when(step == pl.num_programs(0) - 1)
    def _():
        meta = jnp.concatenate([m[...] for m in metas], axis=0).astype(jnp.float32)
        slot, prob, token = routing(meta, expert_ref[0].astype(jnp.float32))
        slots = gate_ref.shape[1]
        hot = one_hot(slot, slots)
        back = place(hot, acc_e[...])
        wide = jnp.broadcast_to(prob, (prob.shape[0], LANES)).astype(jnp.bfloat16)
        slot_prob = dot(hot, wide, ((0,), (0,)))[:, :1]
        up_val = up_ref[0].astype(jnp.float32)
        activated, slope = silu_parts(gate_ref[0].astype(jnp.float32))
        product = back * (activated * up_val)
        ones = jnp.ones((8, product.shape[1]), jnp.float32)
        dots_out[...] = lax.dot_general(
            ones,
            product,
            (((1,), (1,)), ((), ())),
            precision=lax.Precision.HIGHEST,
            preferred_element_type=jnp.float32,
        )[:1]
        scaled = slot_prob * back
        gate_out[0] = (scaled * up_val * slope).astype(jnp.bfloat16)
        up_out[0] = (scaled * activated).astype(jnp.bfloat16)
        dback = place(one_hot(token, dgate_ref.shape[0]), acc_d[...])
        dactivated, dslope = silu_parts(dgate_ref[...].astype(jnp.float32))
        dgate_out[...] = (dback * dup_ref[...].astype(jnp.float32) * dslope).astype(jnp.bfloat16)
        dup_out[...] = (dback * dactivated).astype(jnp.bfloat16)


def ring(count, step):
    return [(i, (i + step) % count) for i in range(count)]


def local(
    grad_out,
    gate_prob,
    expert_ids,
    slot_positions,
    expert_down,
    dense_down,
    expert_gate_pre,
    expert_up_pre,
    dense_gate_pre,
    dense_up_pre,
):
    nx, ny, ne = lax.axis_size("x"), lax.axis_size("y"), lax.axis_size("e")
    expert, part = lax.axis_index("e"), lax.axis_index(("l", "c"))
    tokens, width = grad_out.shape
    slots, hwidth = expert_gate_pre.shape[1:]
    dwidth = dense_gate_pre.shape[1]
    capacity = slots // ne
    eighth = tokens // (RUN * CORES)
    block = width // (nx * ny)
    bf16 = jnp.bfloat16
    stride = -(-(block + 8) // LANES) * LANES
    expert_arr = expert.reshape(1).astype(jnp.int32)
    smem = pl.BlockSpec(memory_space=pltpu.SMEM)
    vmem = pl.BlockSpec(memory_space=pltpu.VMEM)

    hidden = pl.pallas_call(
        hidden_kernel,
        out_shape=jax.ShapeDtypeStruct((ny, SLOT_ROWS + ne * tokens // 4, 4 * LANES), bf16),
        compiler_params=params(),
    )(expert_gate_pre, expert_up_pre, dense_gate_pre, dense_up_pre)

    part_arr = part.reshape(1).astype(jnp.int32)
    span = nx * stride
    mine, cols = pl.pallas_call(
        functools.partial(pick_kernel, capacity, nx, ny),
        out_shape=(
            jax.ShapeDtypeStruct((eighth, width + LANES), bf16),
            jax.ShapeDtypeStruct((ny, eighth, span), bf16),
        ),
        in_specs=[smem] * 2 + [vmem] * 4,
        compiler_params=params(),
    )(expert_arr, part_arr, grad_out, gate_prob.T, expert_ids.T, slot_positions.T)
    cols = lax.all_to_all(cols, "y", split_axis=0, concat_axis=0, tiled=True)
    cols, hidden = lax.optimization_barrier((cols, hidden))
    hiddens = lax.all_to_all(hidden, "y", split_axis=0, concat_axis=0, tiled=True)
    packed = pl.pallas_call(
        pack_kernel,
        out_shape=jax.ShapeDtypeStruct((eighth, ny * span + width + LANES), bf16),
        compiler_params=params(),
    )(cols, mine)
    packed = lax.all_gather(packed, "e", axis=0, tiled=True)
    pieces = [packed] + [lax.ppermute(packed, ("e", "l"), ring(ne * RUN, d)) for d in (1, -1)]
    pieces += [lax.ppermute(p, "c", ring(CORES, 1)) for p in pieces]

    height = hwidth + -(-dwidth // 16) * 16
    ktotal = ny * ne * tokens
    partial_sums = pl.pallas_call(
        functools.partial(weight_kernel, block, ny),
        grid=(1,),
        out_shape=jax.ShapeDtypeStruct((nx, height, stride), bf16),
        in_specs=[smem]
        + [pl.BlockSpec((ne * eighth, ny * span), lambda k: (0, 0))] * 6
        + [whole(*hiddens.shape)],
        out_specs=whole(nx, height, stride),
        scratch_shapes=[
            pltpu.VMEM((ktotal, span), bf16),
            pltpu.VMEM((ktotal, hwidth), bf16),
            pltpu.VMEM((ktotal, LANES), bf16),
        ],
        compiler_params=params(),
    )(expert_arr, *pieces, hiddens)
    partial_sums, expert_arr = lax.optimization_barrier((partial_sums, expert_arr))
    landed = lax.all_to_all(partial_sums, "x", split_axis=0, concat_axis=0, tiled=True)

    depth = math.gcd(ny * span, width)
    base = ny * span // depth
    data_spec = pl.BlockSpec((ne * eighth, depth), lambda k: (0, base + k))
    meta_spec = pl.BlockSpec((ne * eighth, LANES), lambda k: (0, (ny * span + width) // LANES))
    gate_grad, up_grad, dots, dense_gate_grad, dense_up_grad = pl.pallas_call(
        back_kernel,
        grid=(width // depth,),
        out_shape=(
            jax.ShapeDtypeStruct((1, slots, hwidth), bf16),
            jax.ShapeDtypeStruct((1, slots, hwidth), bf16),
            jax.ShapeDtypeStruct((1, slots), jnp.float32),
            jax.ShapeDtypeStruct((ne * tokens, dwidth), bf16),
            jax.ShapeDtypeStruct((ne * tokens, dwidth), bf16),
        ),
        in_specs=[smem]
        + [data_spec] * 6
        + [meta_spec] * 6
        + [
            pl.BlockSpec((1, hwidth, depth), lambda k: (0, 0, k)),
            pl.BlockSpec((dwidth, depth), lambda k: (0, k)),
            whole(1, slots, hwidth),
            whole(1, slots, hwidth),
            whole(ne * tokens, dwidth),
            whole(ne * tokens, dwidth),
        ],
        out_specs=(
            whole(1, slots, hwidth),
            whole(1, slots, hwidth),
            whole(1, slots),
            whole(ne * tokens, dwidth),
            whole(ne * tokens, dwidth),
        ),
        scratch_shapes=[
            pltpu.VMEM((ne * tokens, hwidth), jnp.float32),
            pltpu.VMEM((ne * tokens, dwidth), jnp.float32),
        ],
        compiler_params=params(),
    )(
        expert_arr,
        *pieces,
        *pieces,
        expert_down,
        dense_down,
        expert_gate_pre,
        expert_up_pre,
        dense_gate_pre,
        dense_up_pre,
    )

    all_dots = lax.all_gather(dots, ("l", "c"), axis=0)

    def total(top, count):
        parts = [landed[x, top : top + count, :block].astype(jnp.float32) for x in range(nx)]
        return (sum(parts[1:], parts[0]) * (1.0 / (nx * ny))).astype(bf16)

    expert_down_grad = total(0, hwidth)
    dense_down_grad = total(hwidth, dwidth)
    slot_prob_grad = jnp.sum(all_dots, axis=0)
    return (
        gate_grad,
        up_grad,
        slot_prob_grad,
        expert_down_grad.T[None],
        dense_gate_grad,
        dense_up_grad,
        dense_down_grad.T,
    )


def solution(mesh):
    n_dp, n_expert, n_tensor = (mesh.shape[a] for a in ("dp", "expert", "tensor"))
    fine = Mesh(
        mesh.devices.reshape(X_CHIPS, n_dp // X_CHIPS, n_expert, n_tensor // CORES, CORES),
        ("x", "y", "e", "l", "c"),
    )
    dp, tensor = ("x", "y"), ("l", "c")
    return jax.shard_map(
        local,
        mesh=fine,
        in_specs=(
            P((*dp, "e"), None),
            P((*dp, "e"), None),
            P((*dp, "e"), None),
            P((*dp, "e"), None),
            P("e", tensor, None),
            P(("e", *tensor), None),
            P("e", dp, tensor),
            P("e", dp, tensor),
            P(dp, ("e", *tensor)),
            P(dp, ("e", *tensor)),
        ),
        out_specs=(
            P("e", dp, tensor),
            P("e", dp, tensor),
            P("e", dp),
            P("e", dp, tensor),
            P(dp, ("e", *tensor)),
            P(dp, ("e", *tensor)),
            P(dp, ("e", *tensor)),
        ),
        check_vma=False,
    )
```

```python
import functools

import jax
import jax.numpy as jnp
from jax import lax
from jax.experimental import pallas as pl
from jax.experimental.pallas import tpu as pltpu
from jax.sharding import Mesh
from jax.sharding import PartitionSpec as P

X_CHIPS = 4
RUN = 3
CORES = 2
LANES = 128
SLOT_ROWS = 160
META = 8
VMEM_BYTES = 56 * 1024 * 1024


def silu_parts(gate_val):
    gate_sig = jax.nn.sigmoid(gate_val)
    activated = gate_val * gate_sig
    slope = gate_sig * (1.0 + gate_val * (1.0 - gate_sig))
    return (activated, slope)


def whole(*shape):
    return pl.BlockSpec(shape, lambda *idx: (0,) * len(shape))


def params():
    return pltpu.CompilerParams(vmem_limit_bytes=VMEM_BYTES)


def hidden_kernel(gate_ref, up_ref, dgate_ref, dup_ref, out_ref):
    slots, width = gate_ref.shape[1:]
    tokens, dwidth = dgate_ref.shape
    quarter = tokens // 4
    out_ref[0] = jnp.zeros_like(out_ref[0])
    activated, _ = silu_parts(gate_ref[0].astype(jnp.float32))
    hidden = activated * up_ref[0].astype(jnp.float32)
    pad = jnp.zeros((SLOT_ROWS - slots, width), jnp.float32)
    out_ref[0, :SLOT_ROWS, :width] = jnp.concatenate([hidden, pad], axis=0).astype(jnp.bfloat16)
    dactivated, _ = silu_parts(dgate_ref[...].astype(jnp.float32))
    dhidden = (dactivated * dup_ref[...].astype(jnp.float32)).astype(jnp.bfloat16)
    for j in range(4):
        out_ref[0, SLOT_ROWS : SLOT_ROWS + quarter, j * LANES : j * LANES + dwidth] = dhidden[
            j * quarter : (j + 1) * quarter
        ]
    for y in range(1, out_ref.shape[0]):
        out_ref[y] = out_ref[0]


def pick_kernel(capacity, nx, ny, expert_ref, part_ref, rows_ref, prob_ref, ids_ref, slots_ref, out_ref, cols_ref):
    expert, part = expert_ref[0], part_ref[0]
    eighth = out_ref.shape[0]
    tokens, width = rows_ref.shape
    lane = lax.broadcasted_iota(jnp.int32, (eighth, tokens), 1)
    row = lax.broadcasted_iota(jnp.int32, (eighth, tokens), 0)
    chosen = jnp.where(lane == row + part * eighth, 1.0, 0.0).astype(jnp.bfloat16)
    token = expert * tokens + lax.broadcasted_iota(jnp.int32, (2, tokens), 1)
    meta = jnp.concatenate(
        [
            ids_ref[...].astype(jnp.float32),
            (slots_ref[...] + expert * capacity).astype(jnp.float32),
            prob_ref[...].astype(jnp.float32),
            token.astype(jnp.float32),
        ],
        axis=0,
    ).astype(jnp.bfloat16)
    meta = jnp.concatenate([meta, jnp.zeros((LANES - META, tokens), jnp.bfloat16)], axis=0)
    meta = dot(chosen, meta, ((1,), (1,))).astype(jnp.bfloat16)
    picked = dot(chosen, rows_ref[...], ((1,), (0,))).astype(jnp.bfloat16)
    out_ref[:, :width] = picked
    out_ref[:, width:] = meta
    block = width // (nx * ny)
    for y in range(ny):
        for x in range(nx):
            at = (x * ny + y) * block
            cols_ref[y, :, x * block : (x + 1) * block] = picked[:, at : at + block]
        cols_ref[y, :, nx * block :] = meta


def pack_kernel(cols_ref, rows_ref, out_ref):
    ny, _, total = cols_ref.shape
    span = total - LANES
    width = rows_ref.shape[1] - LANES
    out_ref[:, :width] = rows_ref[:, :width]
    source = lax.broadcasted_iota(jnp.int32, (LANES, LANES), 0)
    target = lax.broadcasted_iota(jnp.int32, (LANES, LANES), 1)
    packed = jnp.zeros((out_ref.shape[0], LANES), jnp.float32)
    for y in range(ny + 1):
        if y < ny:
            out_ref[:, width + y * span : width + (y + 1) * span] = cols_ref[y, :, :span]
        meta = cols_ref[y, :, span:] if y < ny else rows_ref[:, width:]
        moved = (target == source + y * META) & (source < META)
        packed = packed + dot(meta, jnp.where(moved, 1.0, 0.0).astype(jnp.bfloat16), ((1,), (0,)))
    out_ref[:, 2 * width :] = packed.astype(jnp.bfloat16)


def routing(meta, expert):
    hit0 = meta[:, 0:1] == expert
    hit1 = meta[:, 1:2] == expert
    slot = jnp.where(hit0, meta[:, 2:3], jnp.where(hit1, meta[:, 3:4], -1.0)).astype(jnp.int32)
    prob = jnp.where(hit0, meta[:, 4:5], jnp.where(hit1, meta[:, 5:6], 0.0))
    token = meta[:, 6:7].astype(jnp.int32)
    return slot, prob, token


def one_hot(index, count, value=1.0):
    lane = lax.broadcasted_iota(jnp.int32, (index.shape[0], count), 1)
    return jnp.where(lane == index, value, 0.0).astype(jnp.bfloat16)


def dot(a, b, dims):
    return lax.dot_general(a, b, (dims, ((), ())), preferred_element_type=jnp.float32)


def weight_kernel(block, ny, expert_ref, *refs):
    pieces, metas, hid_ref, out_ref, a_ref, be_ref, bd_ref = refs[:6], refs[6:12], *refs[12:17]
    rows, total = pieces[0].shape
    span = total // ny
    group = 6 * rows
    expert = expert_ref[0].astype(jnp.float32)
    width = be_ref.shape[1]
    quarter = hid_ref.shape[1] - SLOT_ROWS
    meta = jnp.concatenate([m[...] for m in metas], axis=0).astype(jnp.float32)
    for y in range(ny):
        top = y * group
        for i, piece in enumerate(pieces):
            a_ref[top + i * rows : top + (i + 1) * rows, :] = piece[:, y * span : (y + 1) * span]
        slot, prob, token = routing(meta[:, y * META : (y + 1) * META], expert)
        weighted = dot(one_hot(slot, SLOT_ROWS, prob), hid_ref[y, :SLOT_ROWS, :width], ((1,), (0,)))
        be_ref[top : top + group, :] = weighted.astype(jnp.bfloat16)
        dense = jnp.concatenate(
            [hid_ref[y, SLOT_ROWS:, j * LANES : (j + 1) * LANES] for j in range(4)], axis=0
        )
        moved = dot(one_hot(token, 4 * quarter), dense, ((1,), (0,)))
        bd_ref[top : top + group, :] = moved.astype(jnp.bfloat16)
    rows_in = a_ref[...]
    nx, height, _ = out_ref.shape
    summed = dot(be_ref[...], rows_in, ((0,), (0,))).astype(jnp.bfloat16)
    dsummed = dot(bd_ref[...], rows_in, ((0,), (0,))).astype(jnp.bfloat16)
    for x in range(nx):
        out_ref[x, :width, :block] = summed[:, x * block : (x + 1) * block]
        out_ref[x, width:, :block] = dsummed[: height - width, x * block : (x + 1) * block]


def place(onehot, values):
    high = values.astype(jnp.bfloat16)
    rest = values - high.astype(jnp.float32)
    middle = rest.astype(jnp.bfloat16)
    low = (rest - middle.astype(jnp.float32)).astype(jnp.bfloat16)
    dims = ((0,), (0,))
    return dot(onehot, high, dims) + dot(onehot, middle, dims) + dot(onehot, low, dims)


def back_kernel(at, expert_ref, *refs):
    datas, metas = refs[:6], refs[6:12]
    we_ref, wd_ref, gate_ref, up_ref, dgate_ref, dup_ref = refs[12:18]
    gate_out, up_out, dots_out, dgate_out, dup_out = refs[18:23]
    acc_e, acc_d = refs[23:25]
    step = pl.program_id(0)

    @pl.when(step == 0)
    def _():
        acc_e[...] = jnp.zeros_like(acc_e)
        acc_d[...] = jnp.zeros_like(acc_d)

    rows = jnp.concatenate([data[...] for data in datas], axis=0)
    acc_e[...] += dot(rows, we_ref[0], ((1,), (1,)))
    acc_d[...] += dot(rows, wd_ref[...], ((1,), (1,)))

    @pl.when(step == pl.num_programs(0) - 1)
    def _():
        meta = jnp.concatenate([m[...] for m in metas], axis=0).astype(jnp.float32)
        slot, prob, token = routing(meta[:, at : at + META], expert_ref[0].astype(jnp.float32))
        slots = gate_ref.shape[1]
        hot = one_hot(slot, slots)
        back = place(hot, acc_e[...])
        wide = jnp.broadcast_to(prob, (prob.shape[0], LANES)).astype(jnp.bfloat16)
        slot_prob = dot(hot, wide, ((0,), (0,)))[:, :1]
        up_val = up_ref[0].astype(jnp.float32)
        activated, slope = silu_parts(gate_ref[0].astype(jnp.float32))
        product = back * (activated * up_val)
        ones = jnp.ones((8, product.shape[1]), jnp.float32)
        dots_out[...] = lax.dot_general(
            ones,
            product,
            (((1,), (1,)), ((), ())),
            precision=lax.Precision.HIGHEST,
            preferred_element_type=jnp.float32,
        )[:1]
        scaled = slot_prob * back
        gate_out[0] = (scaled * up_val * slope).astype(jnp.bfloat16)
        up_out[0] = (scaled * activated).astype(jnp.bfloat16)
        dback = place(one_hot(token, dgate_ref.shape[0]), acc_d[...])
        dactivated, dslope = silu_parts(dgate_ref[...].astype(jnp.float32))
        dgate_out[...] = (dback * dup_ref[...].astype(jnp.float32) * dslope).astype(jnp.bfloat16)
        dup_out[...] = (dback * dactivated).astype(jnp.bfloat16)


def ring(count, step):
    return [(i, (i + step) % count) for i in range(count)]


def local(
    grad_out,
    gate_prob,
    expert_ids,
    slot_positions,
    expert_down,
    dense_down,
    expert_gate_pre,
    expert_up_pre,
    dense_gate_pre,
    dense_up_pre,
):
    nx, ny, ne = lax.axis_size("x"), lax.axis_size("y"), lax.axis_size("e")
    expert, part = lax.axis_index("e"), lax.axis_index(("l", "c"))
    tokens, width = grad_out.shape
    slots, hwidth = expert_gate_pre.shape[1:]
    dwidth = dense_gate_pre.shape[1]
    capacity = slots // ne
    eighth = tokens // (RUN * CORES)
    block = width // (nx * ny)
    bf16 = jnp.bfloat16
    stride = -(-block // LANES) * LANES
    expert_arr = expert.reshape(1).astype(jnp.int32)
    smem = pl.BlockSpec(memory_space=pltpu.SMEM)
    vmem = pl.BlockSpec(memory_space=pltpu.VMEM)

    hidden = pl.pallas_call(
        hidden_kernel,
        out_shape=jax.ShapeDtypeStruct((ny, SLOT_ROWS + ne * tokens // 4, 4 * LANES), bf16),
        compiler_params=params(),
    )(expert_gate_pre, expert_up_pre, dense_gate_pre, dense_up_pre)

    part_arr = part.reshape(1).astype(jnp.int32)
    span = nx * block
    mine, cols = pl.pallas_call(
        functools.partial(pick_kernel, capacity, nx, ny),
        out_shape=(
            jax.ShapeDtypeStruct((eighth, width + LANES), bf16),
            jax.ShapeDtypeStruct((ny, eighth, span + LANES), bf16),
        ),
        in_specs=[smem] * 2 + [vmem] * 4,
        compiler_params=params(),
    )(expert_arr, part_arr, grad_out, gate_prob.T, expert_ids.T, slot_positions.T)
    cols = lax.all_to_all(cols, "y", split_axis=0, concat_axis=0, tiled=True)
    cols, hidden = lax.optimization_barrier((cols, hidden))
    hiddens = lax.all_to_all(hidden, "y", split_axis=0, concat_axis=0, tiled=True)
    packed = pl.pallas_call(
        pack_kernel,
        out_shape=jax.ShapeDtypeStruct((eighth, 2 * width + LANES), bf16),
        compiler_params=params(),
    )(cols, mine)
    packed = lax.all_gather(packed, "e", axis=0, tiled=True)
    pieces = [packed] + [lax.ppermute(packed, ("e", "l"), ring(ne * RUN, d)) for d in (1, -1)]
    pieces += [lax.ppermute(p, "c", ring(CORES, 1)) for p in pieces]

    meta_spec = pl.BlockSpec((ne * eighth, LANES), lambda k: (0, 2 * width // LANES))
    height = hwidth + -(-dwidth // 16) * 16
    ktotal = ny * ne * tokens
    partial_sums = pl.pallas_call(
        functools.partial(weight_kernel, block, ny),
        grid=(1,),
        out_shape=jax.ShapeDtypeStruct((nx, height, stride), bf16),
        in_specs=[smem]
        + [pl.BlockSpec((ne * eighth, width), lambda k: (0, 1))] * 6
        + [meta_spec] * 6
        + [whole(*hiddens.shape)],
        out_specs=whole(nx, height, stride),
        scratch_shapes=[
            pltpu.VMEM((ktotal, span), bf16),
            pltpu.VMEM((ktotal, hwidth), bf16),
            pltpu.VMEM((ktotal, LANES), bf16),
        ],
        compiler_params=params(),
    )(expert_arr, *pieces, *pieces, hiddens)
    partial_sums, expert_arr = lax.optimization_barrier((partial_sums, expert_arr))
    landed = lax.all_to_all(partial_sums, "x", split_axis=0, concat_axis=0, tiled=True)

    depth = width // 2
    data_spec = pl.BlockSpec((ne * eighth, depth), lambda k: (0, k))
    gate_grad, up_grad, dots, dense_gate_grad, dense_up_grad = pl.pallas_call(
        functools.partial(back_kernel, ny * META),
        grid=(width // depth,),
        out_shape=(
            jax.ShapeDtypeStruct((1, slots, hwidth), bf16),
            jax.ShapeDtypeStruct((1, slots, hwidth), bf16),
            jax.ShapeDtypeStruct((1, slots), jnp.float32),
            jax.ShapeDtypeStruct((ne * tokens, dwidth), bf16),
            jax.ShapeDtypeStruct((ne * tokens, dwidth), bf16),
        ),
        in_specs=[smem]
        + [data_spec] * 6
        + [meta_spec] * 6
        + [
            pl.BlockSpec((1, hwidth, depth), lambda k: (0, 0, k)),
            pl.BlockSpec((dwidth, depth), lambda k: (0, k)),
            whole(1, slots, hwidth),
            whole(1, slots, hwidth),
            whole(ne * tokens, dwidth),
            whole(ne * tokens, dwidth),
        ],
        out_specs=(
            whole(1, slots, hwidth),
            whole(1, slots, hwidth),
            whole(1, slots),
            whole(ne * tokens, dwidth),
            whole(ne * tokens, dwidth),
        ),
        scratch_shapes=[
            pltpu.VMEM((ne * tokens, hwidth), jnp.float32),
            pltpu.VMEM((ne * tokens, dwidth), jnp.float32),
        ],
        compiler_params=params(),
    )(
        expert_arr,
        *pieces,
        *pieces,
        expert_down,
        dense_down,
        expert_gate_pre,
        expert_up_pre,
        dense_gate_pre,
        dense_up_pre,
    )

    all_dots = lax.all_gather(dots, ("l", "c"), axis=0)

    def total(top, count):
        parts = [landed[x, top : top + count, :block].astype(jnp.float32) for x in range(nx)]
        return (sum(parts[1:], parts[0]) * (1.0 / (nx * ny))).astype(bf16)

    expert_down_grad = total(0, hwidth)
    dense_down_grad = total(hwidth, dwidth)
    slot_prob_grad = jnp.sum(all_dots, axis=0)
    return (
        gate_grad,
        up_grad,
        slot_prob_grad,
        expert_down_grad.T[None],
        dense_gate_grad,
        dense_up_grad,
        dense_down_grad.T,
    )


def solution(mesh):
    n_dp, n_expert, n_tensor = (mesh.shape[a] for a in ("dp", "expert", "tensor"))
    fine = Mesh(
        mesh.devices.reshape(X_CHIPS, n_dp // X_CHIPS, n_expert, n_tensor // CORES, CORES),
        ("x", "y", "e", "l", "c"),
    )
    dp, tensor = ("x", "y"), ("l", "c")
    return jax.shard_map(
        local,
        mesh=fine,
        in_specs=(
            P((*dp, "e"), None),
            P((*dp, "e"), None),
            P((*dp, "e"), None),
            P((*dp, "e"), None),
            P("e", tensor, None),
            P(("e", *tensor), None),
            P("e", dp, tensor),
            P("e", dp, tensor),
            P(dp, ("e", *tensor)),
            P(dp, ("e", *tensor)),
        ),
        out_specs=(
            P("e", dp, tensor),
            P("e", dp, tensor),
            P("e", dp),
            P("e", dp, tensor),
            P(dp, ("e", *tensor)),
            P(dp, ("e", *tensor)),
            P(dp, ("e", *tensor)),
        ),
        check_vma=False,
    )
```

```python
import functools

import jax
import jax.numpy as jnp
from jax import lax
from jax.experimental import pallas as pl
from jax.experimental.pallas import tpu as pltpu
from jax.sharding import Mesh
from jax.sharding import PartitionSpec as P

X_CHIPS = 4
RUN = 3
CORES = 2
LANES = 128
SLOT_ROWS = 160
META = 8
VMEM_BYTES = 56 * 1024 * 1024


def silu_parts(gate_val):
    gate_sig = jax.nn.sigmoid(gate_val)
    activated = gate_val * gate_sig
    slope = gate_sig * (1.0 + gate_val * (1.0 - gate_sig))
    return (activated, slope)


def whole(*shape):
    return pl.BlockSpec(shape, lambda *idx: (0,) * len(shape))


def params():
    return pltpu.CompilerParams(vmem_limit_bytes=VMEM_BYTES)


def hidden_kernel(gate_ref, up_ref, dgate_ref, dup_ref, out_ref):
    slots, width = gate_ref.shape[1:]
    tokens, dwidth = dgate_ref.shape
    quarter = tokens // 4
    out_ref[0] = jnp.zeros_like(out_ref[0])
    activated, _ = silu_parts(gate_ref[0].astype(jnp.float32))
    hidden = activated * up_ref[0].astype(jnp.float32)
    pad = jnp.zeros((SLOT_ROWS - slots, width), jnp.float32)
    out_ref[0, :SLOT_ROWS, :width] = jnp.concatenate([hidden, pad], axis=0).astype(jnp.bfloat16)
    dactivated, _ = silu_parts(dgate_ref[...].astype(jnp.float32))
    dhidden = (dactivated * dup_ref[...].astype(jnp.float32)).astype(jnp.bfloat16)
    for j in range(4):
        out_ref[0, SLOT_ROWS : SLOT_ROWS + quarter, j * LANES : j * LANES + dwidth] = dhidden[
            j * quarter : (j + 1) * quarter
        ]
    for y in range(1, out_ref.shape[0]):
        out_ref[y] = out_ref[0]


def pick_kernel(capacity, nx, ny, expert_ref, part_ref, rows_ref, prob_ref, ids_ref, slots_ref, out_ref, cols_ref):
    expert, part = expert_ref[0], part_ref[0]
    eighth = out_ref.shape[0]
    tokens, width = rows_ref.shape
    lane = lax.broadcasted_iota(jnp.int32, (eighth, tokens), 1)
    row = lax.broadcasted_iota(jnp.int32, (eighth, tokens), 0)
    chosen = jnp.where(lane == row + part * eighth, 1.0, 0.0).astype(jnp.bfloat16)
    token = expert * tokens + lax.broadcasted_iota(jnp.int32, (2, tokens), 1)
    meta = jnp.concatenate(
        [
            ids_ref[...].astype(jnp.float32),
            (slots_ref[...] + expert * capacity).astype(jnp.float32),
            prob_ref[...].astype(jnp.float32),
            token.astype(jnp.float32),
        ],
        axis=0,
    ).astype(jnp.bfloat16)
    meta = jnp.concatenate([meta, jnp.zeros((LANES - META, tokens), jnp.bfloat16)], axis=0)
    meta = dot(chosen, meta, ((1,), (1,))).astype(jnp.bfloat16)
    picked = dot(chosen, rows_ref[...], ((1,), (0,))).astype(jnp.bfloat16)
    out_ref[:, :width] = picked
    out_ref[:, width:] = meta
    block = width // (nx * ny)
    for y in range(ny):
        for x in range(nx):
            at = (x * ny + y) * block
            cols_ref[y, :, x * block : (x + 1) * block] = picked[:, at : at + block]
        cols_ref[y, :, nx * block :] = meta


def pack_kernel(cols_ref, rows_ref, out_ref):
    ny, _, total = cols_ref.shape
    span = total - LANES
    width = rows_ref.shape[1] - LANES
    out_ref[:, :width] = rows_ref[:, :width]
    source = lax.broadcasted_iota(jnp.int32, (LANES, LANES), 0)
    target = lax.broadcasted_iota(jnp.int32, (LANES, LANES), 1)
    packed = jnp.zeros((out_ref.shape[0], LANES), jnp.float32)
    for y in range(ny + 1):
        if y < ny:
            out_ref[:, width + y * span : width + (y + 1) * span] = cols_ref[y, :, :span]
        meta = cols_ref[y, :, span:] if y < ny else rows_ref[:, width:]
        moved = (target == source + y * META) & (source < META)
        packed = packed + dot(meta, jnp.where(moved, 1.0, 0.0).astype(jnp.bfloat16), ((1,), (0,)))
    out_ref[:, 2 * width :] = packed.astype(jnp.bfloat16)


def routing(meta, expert):
    hit0 = meta[:, 0:1] == expert
    hit1 = meta[:, 1:2] == expert
    slot = jnp.where(hit0, meta[:, 2:3], jnp.where(hit1, meta[:, 3:4], -1.0)).astype(jnp.int32)
    prob = jnp.where(hit0, meta[:, 4:5], jnp.where(hit1, meta[:, 5:6], 0.0))
    token = meta[:, 6:7].astype(jnp.int32)
    return slot, prob, token


def one_hot(index, count, value=1.0):
    lane = lax.broadcasted_iota(jnp.int32, (index.shape[0], count), 1)
    return jnp.where(lane == index, value, 0.0).astype(jnp.bfloat16)


def dot(a, b, dims):
    return lax.dot_general(a, b, (dims, ((), ())), preferred_element_type=jnp.float32)


def weight_kernel(block, ny, expert_ref, *refs):
    pieces, metas, hid_ref, out_ref, a_ref, be_ref, bd_ref = refs[:6], refs[6:12], *refs[12:17]
    rows, total = pieces[0].shape
    span = total // ny
    group = 6 * rows
    expert = expert_ref[0].astype(jnp.float32)
    width = be_ref.shape[1]
    quarter = hid_ref.shape[1] - SLOT_ROWS
    meta = jnp.concatenate([m[...] for m in metas], axis=0).astype(jnp.float32)
    for y in range(ny):
        top = y * group
        for i, piece in enumerate(pieces):
            a_ref[top + i * rows : top + (i + 1) * rows, :] = piece[:, y * span : (y + 1) * span]
        slot, prob, token = routing(meta[:, y * META : (y + 1) * META], expert)
        weighted = dot(one_hot(slot, SLOT_ROWS, prob), hid_ref[y, :SLOT_ROWS, :width], ((1,), (0,)))
        be_ref[top : top + group, :] = weighted.astype(jnp.bfloat16)
        dense = jnp.concatenate(
            [hid_ref[y, SLOT_ROWS:, j * LANES : (j + 1) * LANES] for j in range(4)], axis=0
        )
        moved = dot(one_hot(token, 4 * quarter), dense, ((1,), (0,)))
        bd_ref[top : top + group, :] = moved.astype(jnp.bfloat16)
    rows_in = a_ref[...]
    nx, height, _ = out_ref.shape
    summed = dot(be_ref[...], rows_in, ((0,), (0,))).astype(jnp.bfloat16)
    dsummed = dot(bd_ref[...], rows_in, ((0,), (0,))).astype(jnp.bfloat16)
    for x in range(nx):
        out_ref[x, :width, :block] = summed[:, x * block : (x + 1) * block]
        out_ref[x, width:, :block] = dsummed[: height - width, x * block : (x + 1) * block]


def place(onehot, values):
    high = values.astype(jnp.bfloat16)
    rest = values - high.astype(jnp.float32)
    middle = rest.astype(jnp.bfloat16)
    low = (rest - middle.astype(jnp.float32)).astype(jnp.bfloat16)
    dims = ((0,), (0,))
    return dot(onehot, high, dims) + dot(onehot, middle, dims) + dot(onehot, low, dims)


def back_kernel(at, expert_ref, *refs):
    datas, metas = refs[:6], refs[6:12]
    we_ref, wd_ref, gate_ref, up_ref, dgate_ref, dup_ref = refs[12:18]
    gate_out, up_out, dots_out, dgate_out, dup_out = refs[18:23]
    acc_e, acc_d = refs[23:25]
    step = pl.program_id(0)

    @pl.when(step == 0)
    def _():
        acc_e[...] = jnp.zeros_like(acc_e)
        acc_d[...] = jnp.zeros_like(acc_d)

    rows = jnp.concatenate([data[...] for data in datas], axis=0)
    acc_e[...] += dot(rows, we_ref[0], ((1,), (1,)))
    acc_d[...] += dot(rows, wd_ref[...], ((1,), (1,)))

    @pl.when(step == pl.num_programs(0) - 1)
    def _():
        meta = jnp.concatenate([m[...] for m in metas], axis=0).astype(jnp.float32)
        slot, prob, token = routing(meta[:, at : at + META], expert_ref[0].astype(jnp.float32))
        slots = gate_ref.shape[1]
        hot = one_hot(slot, slots)
        back = place(hot, acc_e[...])
        wide = jnp.broadcast_to(prob, (prob.shape[0], LANES)).astype(jnp.bfloat16)
        slot_prob = dot(hot, wide, ((0,), (0,)))[:, :1]
        up_val = up_ref[0].astype(jnp.float32)
        activated, slope = silu_parts(gate_ref[0].astype(jnp.float32))
        product = back * (activated * up_val)
        ones = jnp.ones((8, product.shape[1]), jnp.float32)
        dots_out[...] = lax.dot_general(
            ones,
            product,
            (((1,), (1,)), ((), ())),
            precision=lax.Precision.HIGHEST,
            preferred_element_type=jnp.float32,
        )[:1]
        scaled = slot_prob * back
        gate_out[0] = (scaled * up_val * slope).astype(jnp.bfloat16)
        up_out[0] = (scaled * activated).astype(jnp.bfloat16)
        dback = place(one_hot(token, dgate_ref.shape[0]), acc_d[...])
        dactivated, dslope = silu_parts(dgate_ref[...].astype(jnp.float32))
        dgate_out[...] = (dback * dup_ref[...].astype(jnp.float32) * dslope).astype(jnp.bfloat16)
        dup_out[...] = (dback * dactivated).astype(jnp.bfloat16)


def ring(count, step):
    return [(i, (i + step) % count) for i in range(count)]


def local(
    grad_out,
    gate_prob,
    expert_ids,
    slot_positions,
    expert_down,
    dense_down,
    expert_gate_pre,
    expert_up_pre,
    dense_gate_pre,
    dense_up_pre,
):
    nx, ny, ne = lax.axis_size("x"), lax.axis_size("y"), lax.axis_size("e")
    expert, part = lax.axis_index("e"), lax.axis_index(("l", "c"))
    tokens, width = grad_out.shape
    slots, hwidth = expert_gate_pre.shape[1:]
    dwidth = dense_gate_pre.shape[1]
    capacity = slots // ne
    eighth = tokens // (RUN * CORES)
    block = width // (nx * ny)
    bf16 = jnp.bfloat16
    stride = -(-block // LANES) * LANES
    expert_arr = expert.reshape(1).astype(jnp.int32)
    smem = pl.BlockSpec(memory_space=pltpu.SMEM)
    vmem = pl.BlockSpec(memory_space=pltpu.VMEM)

    hidden = pl.pallas_call(
        hidden_kernel,
        out_shape=jax.ShapeDtypeStruct((ny, SLOT_ROWS + ne * tokens // 4, 4 * LANES), bf16),
        compiler_params=params(),
    )(expert_gate_pre, expert_up_pre, dense_gate_pre, dense_up_pre)

    part_arr = part.reshape(1).astype(jnp.int32)
    span = nx * block
    mine, cols = pl.pallas_call(
        functools.partial(pick_kernel, capacity, nx, ny),
        out_shape=(
            jax.ShapeDtypeStruct((eighth, width + LANES), bf16),
            jax.ShapeDtypeStruct((ny, eighth, span + LANES), bf16),
        ),
        in_specs=[smem] * 2 + [vmem] * 4,
        compiler_params=params(),
    )(expert_arr, part_arr, grad_out, gate_prob.T, expert_ids.T, slot_positions.T)
    cols = lax.all_to_all(cols, "y", split_axis=0, concat_axis=0, tiled=True)
    cols, hidden = lax.optimization_barrier((cols, hidden))
    hiddens = lax.all_to_all(hidden, "y", split_axis=0, concat_axis=0, tiled=True)
    packed = pl.pallas_call(
        pack_kernel,
        out_shape=jax.ShapeDtypeStruct((eighth, 2 * width + LANES), bf16),
        compiler_params=params(),
    )(cols, mine)
    packed = lax.all_gather(packed, "e", axis=0, tiled=True)
    pieces = [packed] + [lax.ppermute(packed, ("e", "l"), ring(ne * RUN, d)) for d in (1, -1)]
    other = lax.ppermute(packed, "c", ring(CORES, 1))
    pieces[2], other = lax.optimization_barrier((pieces[2], other))
    pieces += [other] + [lax.ppermute(p, "c", ring(CORES, 1)) for p in pieces[1:]]

    meta_spec = pl.BlockSpec((ne * eighth, LANES), lambda k: (0, 2 * width // LANES))
    height = hwidth + -(-dwidth // 16) * 16
    ktotal = ny * ne * tokens
    partial_sums = pl.pallas_call(
        functools.partial(weight_kernel, block, ny),
        grid=(1,),
        out_shape=jax.ShapeDtypeStruct((nx, height, stride), bf16),
        in_specs=[smem]
        + [pl.BlockSpec((ne * eighth, width), lambda k: (0, 1))] * 6
        + [meta_spec] * 6
        + [whole(*hiddens.shape)],
        out_specs=whole(nx, height, stride),
        scratch_shapes=[
            pltpu.VMEM((ktotal, span), bf16),
            pltpu.VMEM((ktotal, hwidth), bf16),
            pltpu.VMEM((ktotal, LANES), bf16),
        ],
        compiler_params=params(),
    )(expert_arr, *pieces, *pieces, hiddens)
    partial_sums, expert_arr = lax.optimization_barrier((partial_sums, expert_arr))
    landed = lax.all_to_all(partial_sums, "x", split_axis=0, concat_axis=0, tiled=True)

    depth = width // 2
    data_spec = pl.BlockSpec((ne * eighth, depth), lambda k: (0, k))
    gate_grad, up_grad, dots, dense_gate_grad, dense_up_grad = pl.pallas_call(
        functools.partial(back_kernel, ny * META),
        grid=(width // depth,),
        out_shape=(
            jax.ShapeDtypeStruct((1, slots, hwidth), bf16),
            jax.ShapeDtypeStruct((1, slots, hwidth), bf16),
            jax.ShapeDtypeStruct((1, slots), jnp.float32),
            jax.ShapeDtypeStruct((ne * tokens, dwidth), bf16),
            jax.ShapeDtypeStruct((ne * tokens, dwidth), bf16),
        ),
        in_specs=[smem]
        + [data_spec] * 6
        + [meta_spec] * 6
        + [
            pl.BlockSpec((1, hwidth, depth), lambda k: (0, 0, k)),
            pl.BlockSpec((dwidth, depth), lambda k: (0, k)),
            whole(1, slots, hwidth),
            whole(1, slots, hwidth),
            whole(ne * tokens, dwidth),
            whole(ne * tokens, dwidth),
        ],
        out_specs=(
            whole(1, slots, hwidth),
            whole(1, slots, hwidth),
            whole(1, slots),
            whole(ne * tokens, dwidth),
            whole(ne * tokens, dwidth),
        ),
        scratch_shapes=[
            pltpu.VMEM((ne * tokens, hwidth), jnp.float32),
            pltpu.VMEM((ne * tokens, dwidth), jnp.float32),
        ],
        compiler_params=params(),
    )(
        expert_arr,
        *pieces,
        *pieces,
        expert_down,
        dense_down,
        expert_gate_pre,
        expert_up_pre,
        dense_gate_pre,
        dense_up_pre,
    )

    all_dots = lax.all_gather(dots, ("l", "c"), axis=0)

    def total(top, count):
        parts = [landed[x, top : top + count, :block].astype(jnp.float32) for x in range(nx)]
        return (sum(parts[1:], parts[0]) * (1.0 / (nx * ny))).astype(bf16)

    expert_down_grad = total(0, hwidth)
    dense_down_grad = total(hwidth, dwidth)
    slot_prob_grad = jnp.sum(all_dots, axis=0)
    return (
        gate_grad,
        up_grad,
        slot_prob_grad,
        expert_down_grad.T[None],
        dense_gate_grad,
        dense_up_grad,
        dense_down_grad.T,
    )


def solution(mesh):
    n_dp, n_expert, n_tensor = (mesh.shape[a] for a in ("dp", "expert", "tensor"))
    fine = Mesh(
        mesh.devices.reshape(X_CHIPS, n_dp // X_CHIPS, n_expert, n_tensor // CORES, CORES),
        ("x", "y", "e", "l", "c"),
    )
    dp, tensor = ("x", "y"), ("l", "c")
    return jax.shard_map(
        local,
        mesh=fine,
        in_specs=(
            P((*dp, "e"), None),
            P((*dp, "e"), None),
            P((*dp, "e"), None),
            P((*dp, "e"), None),
            P("e", tensor, None),
            P(("e", *tensor), None),
            P("e", dp, tensor),
            P("e", dp, tensor),
            P(dp, ("e", *tensor)),
            P(dp, ("e", *tensor)),
        ),
        out_specs=(
            P("e", dp, tensor),
            P("e", dp, tensor),
            P("e", dp),
            P("e", dp, tensor),
            P(dp, ("e", *tensor)),
            P(dp, ("e", *tensor)),
            P(dp, ("e", *tensor)),
        ),
        check_vma=False,
    )
```
